512 devices in a mesh: tm: 32 (over x, y, core), pitch: 16 (over z).
Axes of the slice: x: 4, y: 4, z: 16, core: 2. Of those that a mesh axis runs over, the one named last changes fastest.
Arguments:
- flow: float32 [5, 256, 32768], P(None, 'tm', 'pitch'), may hold values from -6 to 6
- speed: float32 [32768], P('pitch'), may hold values from 0.5 to 2
- rotor_face: float32 [256, 64, 5, 128], P('tm', 'pitch'), may hold values from -6 to 6
- owner: int32 [64, 1], P('pitch'), may hold values from 0 to 15; in each aligned block of 4 rows (0 to 3, 4 to 7, ...) at most 2 rows name the same one
- dest_block: int32 [64], P('pitch'), may hold values from 0 to 15
- intersection: float32 [64], P('pitch'), may hold values from 0.25 to 1
Outputs:
- residual: float32 [5, 256, 32768], P(None, 'tm', 'pitch')
- mean_flow: float32 [5, 32768], P(None, 'pitch')
The draws below stay inside these ranges and needn't reach their ends.
Inputs may be any that keep to these rules, and one draw needn't show every extreme that they name: Among the 4 face blocks of one pitch index no owner is named more than 2 times, a bound that some block reaches.
All inputs are finite; a program needn't handle non-finite values.
Results may differ from the reference program's by a relative error of at most 0.000071.
Values sent between devices are 32-bit elements; how exact they have to be, the bound alone decides.
No kernel may reach another device: no remote copies, remote signals or barrier semaphores. Data moves between devices by JAX's collectives and lax.ppermute only.
A program may use at most 64 MiB of HBM per device.

```python
import math
import jax
import jax.numpy as jnp
import numpy as np
from jax import lax

VARS = 5
NT = 256
CELLS_DEV = 2048
NC = 32768
FACE_DEV = 4
FACES = 64
CAP = 2
N_PITCH = 16


def with_ends(result, own_key, least, largest):
    longest = result.shape.index(max(result.shape))
    spots = []
    for shift in (0, 1):
        where = [jax.random.randint(jax.random.fold_in(own_key, axis), (), 0, length) for axis, length in enumerate(result.shape)]
        where[longest] = (where[longest] + shift) % result.shape[longest]
        spots.append(tuple(where))
    return result.at[spots[0]].set(least).at[spots[1]].set(largest)


def level_of(own_key, dims, split, least, top_value):
    factor_of, own = 1.0, jax.random.fold_in(own_key, 6)
    for axis_at, shards_of in split:
        steps = jnp.exp(jax.random.uniform(jax.random.fold_in(own, axis_at), (shards_of,), jnp.float32, least / len(split), top_value / len(split)))
        factor_of = factor_of * jnp.repeat(steps, dims[axis_at] // shards_of).reshape([-1 if axis == axis_at else 1 for axis in range(len(dims))])
    return factor_of


def routed_block(rng, own, number, rows, number_of, top, limit, slope):
    ranking = jax.random.permutation(rng, number_of)
    heavy_load, ordinary = portions_of(number_of, rows * top, limit, slope, True), portions_of(number_of, rows * top, limit, slope, False)
    places = jnp.arange(number_of)

    def named(sizes, turn):
        used = int((sizes > 0).sum())
        fixed = max(1, used // 4)
        shifted = fixed + (places - fixed + turn * (used - fixed)) % max(1, number_of - fixed)
        return jnp.zeros((number_of,), jnp.int32).at[ranking[jnp.where(places < fixed, places, shifted)]].set(jnp.asarray(sizes, jnp.int32))

    sizes = jnp.where(number % 4 == 0, named(heavy_load, number // 4), named(ordinary, number - number // 4 - 1))
    mixed = jax.random.permutation(jax.random.fold_in(own, 3), number_of)
    giver, taker = mixed[0:number_of // 2 * 2:2], mixed[1:number_of // 2 * 2:2]
    margin = jnp.minimum(sizes[giver] - 1, limit - sizes[taker]) // 2
    margin = jnp.where((giver == ranking[0]) | (taker == ranking[0]) | (sizes[taker] == 0), 0, jnp.maximum(margin, 0))
    shifted = jax.random.randint(jax.random.fold_in(own, 4), (number_of // 2,), 0, 1 << 20) % (margin + 1)
    sizes = sizes.at[giver].add(-shifted).at[taker].add(shifted)
    items = jnp.searchsorted(jnp.cumsum(sizes), jnp.arange(rows * top), side="right").astype(jnp.int32)
    listing = items.reshape(top, rows).T
    listing = listing[jax.random.permutation(jax.random.fold_in(own, 1), rows)]
    turn = jax.random.randint(jax.random.fold_in(own, 2), (rows, 1), 0, top)
    return jnp.take_along_axis(listing, (jnp.arange(top)[None, :] + turn) % top, axis=1)


def portions_of(number_of, total, most, skew, full):
    portions = [(1 << 20) // math.isqrt(grade ** skew) + 1 for grade in range(1, number_of + 1)]
    largest = most if full else min(most, max(-(-total // number_of), total * portions[0] // sum(portions)))
    least = 1 if total - largest >= number_of - 1 else 0
    given, rest = [largest] + [least] * (number_of - 1), total - largest - least * (number_of - 1)
    while rest > 0:
        movable = [i for i in range(1, number_of) if given[i] < largest] or [i for i in range(1, number_of) if given[i] < most]
        whole, left = sum([portions[i] for i in movable]), rest
        for i in movable:
            addition = min(most - given[i], max(1, left * portions[i] // whole), rest)
            given[i] = given[i] + addition
            rest = rest - addition
    return np.array(given)


def noise(stream_key, extent, scale, reach, shards=(), kind=jnp.bfloat16):
    loudness = level_of(stream_key, extent, shards, -0.22, 0.18) if shards else 1.0
    array = jax.random.normal(stream_key, extent, jnp.float32) * scale * loudness
    return jnp.minimum(jnp.maximum(array, -reach), reach).astype(kind)


def setup_inputs(seed: int = 0) -> dict:
    streams_of = jax.random.split(jax.random.key(seed), 7)
    flow = noise(streams_of[0], (VARS, NT, NC), 1.0, 6.0, ((1, 32), (2, 16)), jnp.float32)
    speed = jnp.clip(jnp.exp(math.log(2.0) - 1.3862944 * jax.random.uniform(streams_of[1], (NC,), jnp.float32) ** level_of(streams_of[1], (NC,), ((0, 16),), -0.2, 0.2)), 0.5, 2.0)
    rotor_face = noise(streams_of[2], (NT, FACES, VARS, 128), 1.0, 6.0, ((0, 32), (1, 16)), jnp.float32)
    owner_keys = jax.random.split(jax.random.fold_in(streams_of[3], 1), FACES // FACE_DEV)
    owner_turns = jax.random.permutation(jax.random.fold_in(streams_of[3], 3), FACES // FACE_DEV)
    owner = jax.vmap(lambda own, number: routed_block(jax.random.fold_in(streams_of[3], 2), own, number, FACE_DEV, N_PITCH, 1, CAP, 2))(owner_keys, owner_turns).reshape((FACES, 1))
    dest_block = with_ends(jax.random.randint(streams_of[4], (FACES,), 0, CELLS_DEV // 128), jax.random.fold_in(streams_of[4], 1), 0, (CELLS_DEV // 128) - 1).astype(jnp.int32)
    intersection = jnp.clip(jnp.exp(math.log(1.0) - 1.3862944 * jax.random.uniform(streams_of[5], (FACES,), jnp.float32) ** level_of(streams_of[5], (FACES,), ((0, 16),), -0.2, 0.2)), 0.25, 1.0)
    return {"flow": flow, "speed": speed, "rotor_face": rotor_face, "owner": owner, "dest_block": dest_block, "intersection": intersection}


def spectral_matrix(rows, cols, count):
    gap = (rows[:, None] - cols[None, :]) % count
    safe = jnp.where(gap == 0, 1, gap).astype(jnp.float32)
    angle = jnp.float32(jnp.pi) * safe / count
    parity = (1 - 2 * (gap % 2)).astype(jnp.float32)
    value = (jnp.float32(jnp.pi) / count) * parity * jnp.cos(angle) / jnp.sin(angle)
    return jnp.where(gap == 0, jnp.float32(0.0), value)


def reference(flow, speed, rotor_face, owner, dest_block, intersection):
    count = flow.shape[1]
    index = jnp.arange(count, dtype=jnp.int32)
    spectral = spectral_matrix(index, index, count)
    derivative = jnp.einsum("ts,vsc->vtc", spectral, flow, precision=lax.Precision.HIGHEST)
    mean_flow = jnp.sum(flow, axis=1) / count
    convective = -speed[None, None, :] * (jnp.roll(flow, -1, 2) - jnp.roll(flow, 1, 2)) * 0.5
    nblocks = flow.shape[2] // 128
    target = owner[:, 0] * (CELLS_DEV // 128) + dest_block
    weighted = intersection[None, :, None, None] * rotor_face
    hits = (target[:, None] == jnp.arange(nblocks, dtype=jnp.int32)[None, :]).astype(jnp.float32)
    inject = jnp.einsum("fb,tfvj->vtbj", hits, weighted, precision=lax.Precision.HIGHEST)
    inject = inject.reshape(flow.shape)
    residual = derivative + convective + inject
    return residual, mean_flow
```

```python
import jax
import jax.numpy as jnp
from jax import lax
from jax.experimental import pallas as pl
from jax.experimental.pallas import tpu as pltpu
from jax.sharding import PartitionSpec as P

LANES = 128
ROWS = 8
META = 8
OWNER_AT, DEST_AT = 16, 24
VMEM = 32 * 1024 * 1024
NEAR = (1, -1)
RELAYED = (3, -3, 6, -6)
DIRECT = (8,)


def vmem():
    return pl.BlockSpec(memory_space=pltpu.VMEM)


def smem():
    return pl.BlockSpec(memory_space=pltpu.SMEM)


def call(body, outs, in_specs, scratch=(), flops=0, moved=0):
    return pl.pallas_call(
        body,
        out_shape=outs,
        in_specs=in_specs,
        out_specs=jax.tree.map(lambda _: vmem(), outs),
        scratch_shapes=list(scratch),
        compiler_params=pltpu.CompilerParams(vmem_limit_bytes=VMEM),
        cost_estimate=pl.CostEstimate(flops=flops, bytes_accessed=moved, transcendentals=0),
    )


def f32(*shape):
    return jax.ShapeDtypeStruct(shape, jnp.float32)


def cells_out_kernel(flow_ref, out_ref):
    nvars, _, cells = flow_ref.shape
    per = cells // LANES
    tiles = nvars * per
    row = lax.broadcasted_iota(jnp.int32, (ROWS, LANES), 0)
    sums = None
    for m in range(tiles):
        v, c = divmod(m, per)
        tile = flow_ref[v, :, c * LANES : (c + 1) * LANES]
        out_ref[m * ROWS : (m + 1) * ROWS, :] = tile
        total = jnp.sum(tile, axis=0, keepdims=True)
        total = jnp.broadcast_to(total, (ROWS, LANES))
        sums = total if m % ROWS == 0 else jnp.where(row == m % ROWS, total, sums)
        if m % ROWS == ROWS - 1:
            q = tiles + m // ROWS
            out_ref[q * ROWS : (q + 1) * ROWS, :] = sums
    used = (tiles + tiles // ROWS) * ROWS
    rest = out_ref.shape[0] - used
    out_ref[used:, :] = jnp.zeros((rest, LANES), jnp.float32)


def weigh_kernel(owner_ref, dest_ref, weight_ref, flow_ref, rotor_ref, *out_refs):
    mine_ref, direct_refs = out_refs[0], out_refs[1:]
    nvars, _, cells = flow_ref.shape
    faces = weight_ref.shape[0]
    block = nvars * ROWS
    me = lax.axis_index("pitch")
    count = lax.axis_size("pitch")
    lane = lax.broadcasted_iota(jnp.int32, (ROWS, LANES), 1)
    meta = jnp.zeros((ROWS, LANES), jnp.float32)
    for v in range(nvars):
        tail = pltpu.roll(flow_ref[v, :, cells - LANES :], v + 1, 1)
        head = pltpu.roll(flow_ref[v, :, :LANES], nvars + v, 1)
        meta = jnp.where(lane == v, tail, meta)
        meta = jnp.where(lane == nvars + v, head, meta)
    for f in range(faces):
        meta = jnp.where(lane == OWNER_AT + f, owner_ref[f].astype(jnp.float32), meta)
        meta = jnp.where(lane == DEST_AT + f, dest_ref[f].astype(jnp.float32), meta)
        for v in range(nvars):
            rows = rotor_ref[pl.ds(v * faces + f, ROWS, stride=nvars * faces), :]
            at = f * block + v * ROWS
            mine_ref[at : at + ROWS, :] = weight_ref[f] * rows
    mine_ref[faces * block :, :] = meta
    for offset, out_ref in zip(DIRECT, direct_refs):
        route(
            [(mine_ref, f * block, owner_ref[f], dest_ref[f]) for f in range(faces)],
            lax.rem(me + (offset + count), count),
            block,
            out_ref,
        )


def route(items, target, block, out_ref):
    lane = lax.broadcasted_iota(jnp.int32, (META, LANES), 1)
    slots = (out_ref.shape[0] - META) // block
    meta = jnp.full((META, LANES), -1.0, jnp.float32)
    used = jnp.int32(0)
    for ref, at, owner, dest in items:
        hit = owner == target

        @pl.when(hit)
        def _(ref=ref, at=at, used=used):
            to = pl.multiple_of(used * block, block)
            out_ref[pl.ds(to, block), :] = ref[at : at + block, :]

        where = jnp.where(hit, DEST_AT + used, -1)
        meta = jnp.where(lane == where, dest.astype(jnp.float32), meta)
        used = used + hit.astype(jnp.int32)
    out_ref[slots * block :, :] = meta


def fetch_ids(refs, ids_ref, sems):
    copies = [
        pltpu.make_async_copy(ref.at[pl.ds(ref.shape[0] - META, META), :], ids_ref.at[i], sems.at[i])
        for i, ref in enumerate(refs)
    ]
    for copy in copies:
        copy.start()

    def wait():
        for copy in copies:
            copy.wait()

    return wait


def id_scratch(groups):
    return [pltpu.SMEM((groups, META, LANES), jnp.float32), pltpu.SemaphoreType.DMA((groups,))]


def received(faces, block, refs, ids_ref):
    items = []
    for i, ref in enumerate(refs):
        for f in range(faces):
            ids = [ids_ref[i, 0, at + f].astype(jnp.int32) for at in (OWNER_AT, DEST_AT)]
            items.append((ref, f * block, *ids))
    return items


def relay_kernel(owner_ref, dest_ref, mine_ref, below_ref, above_ref, *rest):
    out_refs, ids_ref, sems = rest[:-2], rest[-2], rest[-1]
    wait = fetch_ids((below_ref, above_ref), ids_ref, sems)
    faces = owner_ref.shape[0]
    block = (mine_ref.shape[0] - META) // faces
    me = lax.axis_index("pitch")
    count = lax.axis_size("pitch")
    items = []
    for f in range(faces):
        items.append((mine_ref, f * block, owner_ref[f], dest_ref[f]))
    wait()
    items += received(faces, block, (below_ref, above_ref), ids_ref)
    for offset, out_ref in zip(RELAYED, out_refs):
        route(items, lax.rem(me + (offset + count), count), block, out_ref)


def add_block(out_ref, ref, at, dest):
    nvars = out_ref.shape[0]
    to = pl.ds(pl.multiple_of(dest * LANES, LANES), LANES)
    for v in range(nvars):
        out_ref[v, :, to] += ref[at + v * ROWS : at + (v + 1) * ROWS, :]


def base_kernel(owner_ref, dest_ref, flow_ref, speed_ref, mine_ref, below_ref, above_ref, out_ref, ids_ref, sems):
    wait = fetch_ids((below_ref, above_ref), ids_ref, sems)
    nvars, _, cells = flow_ref.shape
    faces = owner_ref.shape[0]
    block = nvars * ROWS
    per = cells // LANES
    me = lax.axis_index("pitch")
    lane = lax.broadcasted_iota(jnp.int32, (ROWS, LANES), 1)
    before, after = below_ref[faces * block :, :], above_ref[faces * block :, :]
    for v in range(nvars):
        left_edge = pltpu.roll(before, (LANES - v) % LANES, 1)
        right_edge = pltpu.roll(after, LANES - 1 - nvars - v, 1)
        tiles = [flow_ref[v, :, c * LANES : (c + 1) * LANES] for c in range(per)]
        downs = [pltpu.roll(tile, 1, 1) for tile in tiles]
        ups = [pltpu.roll(tile, LANES - 1, 1) for tile in tiles]
        for c in range(per):
            down = jnp.where(lane == 0, left_edge if c == 0 else downs[c - 1], downs[c])
            up = jnp.where(lane == LANES - 1, right_edge if c == per - 1 else ups[c + 1], ups[c])
            speed = speed_ref[c : c + 1, :]
            out_ref[v, :, c * LANES : (c + 1) * LANES] = -speed * (up - down) * 0.5
    items = [(mine_ref, f * block, owner_ref[f], dest_ref[f]) for f in range(faces)]
    wait()
    items += received(faces, block, (below_ref, above_ref), ids_ref)
    for ref, at, owner, dest in items:

        @pl.when(owner == me)
        def _(ref=ref, at=at, dest=dest):
            add_block(out_ref, ref, at, dest)


def spectral_kernel(matrix_ref, cells_ref, out_ref, *, first_mean, last_mean):
    count = matrix_ref.shape[0]
    devs = count // ROWS
    slots = cells_ref.shape[0] // count
    me = lax.axis_index("tm")
    got = cells_ref[...].reshape(devs, slots, ROWS, LANES)
    columns = jnp.concatenate([got[:, k].reshape(count, LANES) for k in range(slots)], axis=1)
    product = jnp.dot(matrix_ref[...], columns, precision=lax.Precision.HIGHEST, preferred_element_type=jnp.float32)
    for k in range(slots):
        tile = me * slots + k
        is_mean = jnp.logical_and(tile >= first_mean, tile < last_mean)
        mean = jnp.sum(got[:, k], axis=0) / count
        for d in range(devs):
            part = product[d * ROWS : (d + 1) * ROWS, k * LANES : (k + 1) * LANES]
            at = (d * slots + k) * ROWS
            out_ref[at : at + ROWS, :] = jnp.where(is_mean, mean, part)


def finish_kernel(*refs):
    base_ref, cells_ref, blocks = refs[0], refs[1], refs[2:-4]
    out_ref, mean_ref, ids_ref, sems = refs[-4:]
    wait = fetch_ids(blocks, ids_ref, sems)
    nvars, _, cells = out_ref.shape
    block = nvars * ROWS
    per = cells // LANES
    for m in range(nvars * per):
        v, c = divmod(m, per)
        at = slice(c * LANES, (c + 1) * LANES)
        out_ref[v, :, at] = cells_ref[m * ROWS : (m + 1) * ROWS, :] + base_ref[v, :, at]
        row = nvars * per * ROWS + m
        mean_ref[v : v + 1, at] = cells_ref[row : row + 1, :]
    wait()
    for i, ref in enumerate(blocks):
        for slot in range((ref.shape[0] - META) // block):
            dest = ids_ref[i, 0, DEST_AT + slot].astype(jnp.int32)

            @pl.when(dest >= 0)
            def _(ref=ref, slot=slot, dest=dest):
                add_block(out_ref, ref, slot * block, dest)


def spectral_matrix(count):
    index = jnp.arange(count, dtype=jnp.int32)
    gap = (index[:, None] - index[None, :]) % count
    safe = jnp.where(gap == 0, 1, gap).astype(jnp.float32)
    angle = jnp.float32(jnp.pi) * safe / count
    parity = (1 - 2 * (gap % 2)).astype(jnp.float32)
    value = jnp.float32(jnp.pi) / count * parity * jnp.cos(angle) / jnp.sin(angle)
    return jnp.where(gap == 0, jnp.float32(0.0), value)


def shifted(array, by):
    count = lax.axis_size("pitch")
    return lax.ppermute(array, "pitch", [(i, (i + by) % count) for i in range(count)])


def per_device(flow, speed, rotor_face, owner, dest_block, intersection):
    nvars, inst, cells = flow.shape
    faces = rotor_face.shape[1]
    devs = lax.axis_size("tm")
    count = inst * devs
    block = nvars * inst
    tiles = nvars * cells // LANES
    slots = -(-(tiles + tiles // ROWS) // devs)
    owner = owner.reshape(faces)
    rotor = jnp.transpose(rotor_face, (0, 2, 1, 3)).reshape(inst * nvars * faces, LANES)
    speed = speed.reshape(cells // LANES, LANES)

    packed = call(cells_out_kernel, f32(devs * slots * ROWS, LANES), [vmem()], moved=700_000)(flow)
    mine, *direct = call(
        weigh_kernel,
        [f32(faces * block + META, LANES)] + [f32(2 * block + META, LANES) for _ in DIRECT],
        [smem(), smem(), smem(), vmem(), vmem()],
        moved=600_000,
    )(owner, dest_block, intersection, flow, rotor)
    by_cell = lax.all_to_all(packed, "tm", 0, 0, tiled=True)
    below, above = shifted(mine, 1), shifted(mine, -1)
    relays = call(
        relay_kernel,
        [f32(6 * block + META, LANES) for _ in RELAYED],
        [smem(), smem(), vmem(), vmem(), vmem()],
        id_scratch(2),
        moved=700_000,
    )(owner, dest_block, mine, below, above)
    by_cell, relays = lax.optimization_barrier((by_cell, relays))
    sent = [shifted(a, by) for a, by in zip(relays, RELAYED)]
    sent += [shifted(a, by) for a, by in zip(direct, DIRECT)]
    base = call(
        base_kernel,
        f32(nvars, inst, cells),
        [smem(), smem(), vmem(), vmem(), vmem(), vmem(), vmem()],
        id_scratch(2),
        moved=900_000,
    )(owner, dest_block, flow, speed, mine, below, above)

    def spectral(matrix_ref, cells_ref, out_ref):
        spectral_kernel(matrix_ref, cells_ref, out_ref, first_mean=tiles, last_mean=tiles + tiles // ROWS)

    product = call(spectral, f32(devs * slots * ROWS, LANES), [vmem(), vmem()], flops=6 * 2 * count * count * slots * LANES, moved=1_000_000)(
        spectral_matrix(count), by_cell
    )
    by_time = lax.all_to_all(product, "tm", 0, 0, tiled=True)
    residual, mean_flow = call(
        finish_kernel,
        (f32(nvars, inst, cells), f32(nvars, cells)),
        [vmem()] * (2 + len(sent)),
        id_scratch(len(sent)),
        moved=1_500_000,
    )(base, by_time, *sent)
    return residual, mean_flow


def solution(mesh):
    placed = (
        P(None, "tm", "pitch"),
        P("pitch"),
        P("tm", "pitch", None, None),
        P("pitch", None),
        P("pitch"),
        P("pitch"),
    )
    return jax.shard_map(
        per_device,
        mesh=mesh,
        in_specs=placed,
        out_specs=(P(None, "tm", "pitch"), P(None, "pitch")),
        check_vma=False,
    )
```

```python
import functools

import jax
import jax.numpy as jnp
from jax import lax
from jax.experimental import pallas as pl
from jax.experimental.pallas import tpu as pltpu
from jax.sharding import PartitionSpec as P

LANES = 128
ROWS = 8
META = 8
OWNER_AT, DEST_AT = 16, 24
VMEM = 32 * 1024 * 1024
CAP = 2
CLASSES = 4


def vmem():
    return pl.BlockSpec(memory_space=pltpu.VMEM)


def smem():
    return pl.BlockSpec(memory_space=pltpu.SMEM)


def call(body, outs, in_specs, scratch=(), flops=0, moved=0):
    return pl.pallas_call(
        body,
        out_shape=outs,
        in_specs=in_specs,
        out_specs=jax.tree.map(lambda _: vmem(), outs),
        scratch_shapes=list(scratch),
        compiler_params=pltpu.CompilerParams(vmem_limit_bytes=VMEM),
        cost_estimate=pl.CostEstimate(flops=flops, bytes_accessed=moved, transcendentals=0),
    )


def f32(*shape):
    return jax.ShapeDtypeStruct(shape, jnp.float32)


def cells_out_kernel(flow_ref, out_ref):
    nvars, _, cells = flow_ref.shape
    per = cells // LANES
    tiles = nvars * per
    row = lax.broadcasted_iota(jnp.int32, (ROWS, LANES), 0)
    sums = None
    for m in range(tiles):
        v, c = divmod(m, per)
        tile = flow_ref[v, :, c * LANES : (c + 1) * LANES]
        out_ref[m * ROWS : (m + 1) * ROWS, :] = tile
        total = jnp.sum(tile, axis=0, keepdims=True)
        total = jnp.broadcast_to(total, (ROWS, LANES))
        sums = total if m % ROWS == 0 else jnp.where(row == m % ROWS, total, sums)
        if m % ROWS == ROWS - 1:
            q = tiles + m // ROWS
            out_ref[q * ROWS : (q + 1) * ROWS, :] = sums
    used = (tiles + tiles // ROWS) * ROWS
    rest = out_ref.shape[0] - used
    out_ref[used:, :] = jnp.zeros((rest, LANES), jnp.float32)


def weigh_kernel(owner_ref, dest_ref, weight_ref, flow_ref, rotor_ref, mine_ref):
    nvars, _, cells = flow_ref.shape
    faces = weight_ref.shape[0]
    block = nvars * ROWS
    lane = lax.broadcasted_iota(jnp.int32, (ROWS, LANES), 1)
    meta = jnp.zeros((ROWS, LANES), jnp.float32)
    for v in range(nvars):
        tail = pltpu.roll(flow_ref[v, :, cells - LANES :], v + 1, 1)
        head = pltpu.roll(flow_ref[v, :, :LANES], nvars + v, 1)
        meta = jnp.where(lane == v, tail, meta)
        meta = jnp.where(lane == nvars + v, head, meta)
    for f in range(faces):
        meta = jnp.where(lane == OWNER_AT + f, owner_ref[f].astype(jnp.float32), meta)
        meta = jnp.where(lane == DEST_AT + f, dest_ref[f].astype(jnp.float32), meta)
        for v in range(nvars):
            rows = rotor_ref[pl.ds(v * faces + f, ROWS, stride=nvars * faces), :]
            at = f * block + v * ROWS
            mine_ref[at : at + ROWS, :] = weight_ref[f] * rows
    mine_ref[faces * block :, :] = meta


def route(items, target, halo, block, out_ref):
    lane = lax.broadcasted_iota(jnp.int32, (META, LANES), 1)
    slots = (out_ref.shape[0] - META) // block
    meta = jnp.where(lane < OWNER_AT, halo, -1.0)
    used = jnp.int32(0)
    for ref, at, owner, dest in items:
        hit = owner == target

        @pl.when(hit)
        def _(ref=ref, at=at, used=used):
            to = pl.multiple_of(used * block, block)
            out_ref[pl.ds(to, block), :] = ref[at : at + block, :]

        where = jnp.where(hit, DEST_AT + used, -1)
        meta = jnp.where(lane == where, dest.astype(jnp.float32), meta)
        used = used + hit.astype(jnp.int32)
    out_ref[slots * block :, :] = meta


def fetch_ids(parts, ids_ref, sems):
    copies = [
        pltpu.make_async_copy(ref.at[pl.ds(at, META), :], ids_ref.at[i], sems.at[i])
        for i, (ref, at) in enumerate(parts)
    ]
    for copy in copies:
        copy.start()

    def wait():
        for copy in copies:
            copy.wait()

    return wait


def id_scratch(groups):
    return [pltpu.SMEM((groups, META, LANES), jnp.float32), pltpu.SemaphoreType.DMA((groups,))]


def metas_of_group(group_ref, rows):
    return [(group_ref, at + rows - META) for at in range(0, group_ref.shape[0], rows)]


def blocks_of_group(group_ref, rows, block, ids_ref):
    items = []
    for i, at in enumerate(range(0, group_ref.shape[0], rows)):
        for f in range((rows - META) // block):
            ids = [ids_ref[i, 0, lane + f].astype(jnp.int32) for lane in (OWNER_AT, DEST_AT)]
            items.append((group_ref, at + f * block, *ids))
    return items


def hops(plane):
    side = 2 * (plane % 2) - 1
    return [1, -1] + [side * by for by in range(2, CLASSES - 1)]


def relay_kernel(mine_ref, group_ref, *refs, block):
    out_refs, ids_ref, sems = refs[:-2], refs[-2], refs[-1]
    rows = mine_ref.shape[0]
    fetch_ids(metas_of_group(group_ref, rows), ids_ref, sems)()
    me = lax.axis_index("pitch")
    count = lax.axis_size("pitch")
    halo = mine_ref[rows - META :, :]
    items = blocks_of_group(group_ref, rows, block, ids_ref)
    for by, out_ref in zip(hops(me), out_refs):
        route(items, lax.rem(me + count + by, count), halo, block, out_ref)


def add_block(out_ref, ref, at, dest):
    nvars = out_ref.shape[0]
    to = pl.ds(pl.multiple_of(dest * LANES, LANES), LANES)
    for v in range(nvars):
        out_ref[v, :, to] += ref[at + v * ROWS : at + (v + 1) * ROWS, :]


def base_kernel(flow_ref, speed_ref, group_ref, below_ref, above_ref, out_ref, ids_ref, sems, *, rows):
    wait = fetch_ids(metas_of_group(group_ref, rows), ids_ref, sems)
    nvars, _, cells = flow_ref.shape
    block = nvars * ROWS
    per = cells // LANES
    me = lax.axis_index("pitch")
    lane = lax.broadcasted_iota(jnp.int32, (ROWS, LANES), 1)
    before, after = [ref[ref.shape[0] - META :, :] for ref in (below_ref, above_ref)]
    for v in range(nvars):
        left_edge = pltpu.roll(before, (LANES - v) % LANES, 1)
        right_edge = pltpu.roll(after, LANES - 1 - nvars - v, 1)
        tiles = [flow_ref[v, :, c * LANES : (c + 1) * LANES] for c in range(per)]
        downs = [pltpu.roll(tile, 1, 1) for tile in tiles]
        ups = [pltpu.roll(tile, LANES - 1, 1) for tile in tiles]
        for c in range(per):
            down = jnp.where(lane == 0, left_edge if c == 0 else downs[c - 1], downs[c])
            up = jnp.where(lane == LANES - 1, right_edge if c == per - 1 else ups[c + 1], ups[c])
            speed = speed_ref[c : c + 1, :]
            out_ref[v, :, c * LANES : (c + 1) * LANES] = -speed * (up - down) * 0.5
    wait()
    items = blocks_of_group(group_ref, rows, block, ids_ref)
    for ref, at, owner, dest in items:

        @pl.when(owner == me)
        def _(ref=ref, at=at, dest=dest):
            add_block(out_ref, ref, at, dest)


def spectral_kernel(matrix_ref, cells_ref, out_ref, *, first_mean, last_mean):
    count = matrix_ref.shape[0]
    devs = count // ROWS
    slots = cells_ref.shape[0] // count
    me = lax.axis_index("tm")
    got = cells_ref[...].reshape(devs, slots, ROWS, LANES)
    columns = jnp.concatenate([got[:, k].reshape(count, LANES) for k in range(slots)], axis=1)
    product = jnp.dot(matrix_ref[...], columns, precision=lax.Precision.HIGHEST, preferred_element_type=jnp.float32)
    for k in range(slots):
        tile = me * slots + k
        is_mean = jnp.logical_and(tile >= first_mean, tile < last_mean)
        mean = jnp.sum(got[:, k], axis=0) / count
        for d in range(devs):
            part = product[d * ROWS : (d + 1) * ROWS, k * LANES : (k + 1) * LANES]
            at = (d * slots + k) * ROWS
            out_ref[at : at + ROWS, :] = jnp.where(is_mean, mean, part)


def finish_kernel(*refs):
    base_ref, cells_ref, blocks = refs[0], refs[1], refs[2:-4]
    out_ref, mean_ref, ids_ref, sems = refs[-4:]
    wait = fetch_ids([(ref, ref.shape[0] - META) for ref in blocks], ids_ref, sems)
    nvars, _, cells = out_ref.shape
    block = nvars * ROWS
    per = cells // LANES
    for m in range(nvars * per):
        v, c = divmod(m, per)
        at = slice(c * LANES, (c + 1) * LANES)
        out_ref[v, :, at] = cells_ref[m * ROWS : (m + 1) * ROWS, :] + base_ref[v, :, at]
        row = nvars * per * ROWS + m
        mean_ref[v : v + 1, at] = cells_ref[row : row + 1, :]
    wait()
    for i, ref in enumerate(blocks):
        for slot in range((ref.shape[0] - META) // block):
            dest = ids_ref[i, 0, DEST_AT + slot].astype(jnp.int32)

            @pl.when(dest >= 0)
            def _(ref=ref, slot=slot, dest=dest):
                add_block(out_ref, ref, slot * block, dest)


def spectral_matrix(count):
    index = jnp.arange(count, dtype=jnp.int32)
    gap = (index[:, None] - index[None, :]) % count
    safe = jnp.where(gap == 0, 1, gap).astype(jnp.float32)
    angle = jnp.float32(jnp.pi) * safe / count
    parity = (1 - 2 * (gap % 2)).astype(jnp.float32)
    value = jnp.float32(jnp.pi) / count * parity * jnp.cos(angle) / jnp.sin(angle)
    return jnp.where(gap == 0, jnp.float32(0.0), value)


def forwarded(array, i):
    count = lax.axis_size("pitch")
    return lax.ppermute(array, "pitch", [(p, (p + hops(p)[i]) % count) for p in range(count)])


def per_device(flow, speed, rotor_face, owner, dest_block, intersection):
    nvars, inst, cells = flow.shape
    faces = rotor_face.shape[1]
    devs = lax.axis_size("tm")
    count = inst * devs
    block = nvars * inst
    tiles = nvars * cells // LANES
    slots = -(-(tiles + tiles // ROWS) // devs)
    owner = owner.reshape(faces)
    rotor = jnp.transpose(rotor_face, (0, 2, 1, 3)).reshape(inst * nvars * faces, LANES)
    speed = speed.reshape(cells // LANES, LANES)

    packed = call(cells_out_kernel, f32(devs * slots * ROWS, LANES), [vmem()], moved=700_000)(flow)
    mine = call(
        weigh_kernel,
        f32(faces * block + META, LANES),
        [smem(), smem(), smem(), vmem(), vmem()],
        moved=600_000,
    )(owner, dest_block, intersection, flow, rotor)
    by_cell = lax.all_to_all(packed, "tm", 0, 0, tiled=True)
    planes = lax.axis_size("pitch")
    rows = faces * block + META
    classes = [list(range(i, planes, CLASSES)) for i in range(CLASSES)]
    members = planes // CLASSES
    group = lax.all_gather(mine, "pitch", tiled=True, axis_index_groups=classes)
    relays = call(
        functools.partial(relay_kernel, block=block),
        [f32(members * CAP * block + META, LANES) for _ in range(CLASSES - 1)],
        [vmem(), vmem()],
        id_scratch(members),
        moved=1_500_000,
    )(mine, group)
    by_cell, relays = lax.optimization_barrier((by_cell, relays))
    sent = [forwarded(a, i) for i, a in enumerate(relays)]
    base = call(
        functools.partial(base_kernel, rows=rows),
        f32(nvars, inst, cells),
        [vmem()] * 5,
        id_scratch(members),
        moved=900_000,
    )(flow, speed, group, sent[0], sent[1])

    def spectral(matrix_ref, cells_ref, out_ref):
        spectral_kernel(matrix_ref, cells_ref, out_ref, first_mean=tiles, last_mean=tiles + tiles // ROWS)

    product = call(spectral, f32(devs * slots * ROWS, LANES), [vmem(), vmem()], flops=6 * 2 * count * count * slots * LANES, moved=1_000_000)(
        spectral_matrix(count), by_cell
    )
    by_time = lax.all_to_all(product, "tm", 0, 0, tiled=True)
    residual, mean_flow = call(
        finish_kernel,
        (f32(nvars, inst, cells), f32(nvars, cells)),
        [vmem()] * (2 + len(sent)),
        id_scratch(len(sent)),
        moved=1_500_000,
    )(base, by_time, *sent)
    return residual, mean_flow


def solution(mesh):
    placed = (
        P(None, "tm", "pitch"),
        P("pitch"),
        P("tm", "pitch", None, None),
        P("pitch", None),
        P("pitch"),
        P("pitch"),
    )
    return jax.shard_map(
        per_device,
        mesh=mesh,
        in_specs=placed,
        out_specs=(P(None, "tm", "pitch"), P(None, "pitch")),
        check_vma=False,
    )
```

```python
import functools

import jax
import jax.numpy as jnp
from jax import lax
from jax.experimental import pallas as pl
from jax.experimental.pallas import tpu as pltpu
from jax.sharding import PartitionSpec as P

LANES = 128
ROWS = 8
META = 8
OWNER_AT, DEST_AT = 16, 24
VMEM = 32 * 1024 * 1024
SLOW = 20_000_000_000
CAP = 2
FAR, NEAR = 3, 3


def vmem():
    return pl.BlockSpec(memory_space=pltpu.VMEM)


def smem():
    return pl.BlockSpec(memory_space=pltpu.SMEM)


def call(body, outs, in_specs, scratch=(), flops=0, moved=0):
    return pl.pallas_call(
        body,
        out_shape=outs,
        in_specs=in_specs,
        out_specs=jax.tree.map(lambda _: vmem(), outs),
        scratch_shapes=list(scratch),
        compiler_params=pltpu.CompilerParams(vmem_limit_bytes=VMEM),
        cost_estimate=pl.CostEstimate(flops=flops, bytes_accessed=moved, transcendentals=0),
    )


def f32(*shape):
    return jax.ShapeDtypeStruct(shape, jnp.float32)


def pack_kernel(flow_ref, out_ref):
    nvars, _, cells = flow_ref.shape
    per = cells // LANES
    tiles = nvars * per
    row = lax.broadcasted_iota(jnp.int32, (ROWS, LANES), 0)
    sums = None
    for m in range(tiles):
        v, c = divmod(m, per)
        tile = flow_ref[v, :, c * LANES : (c + 1) * LANES]
        out_ref[m * ROWS : (m + 1) * ROWS, :] = tile
        total = jnp.sum(tile, axis=0, keepdims=True)
        total = jnp.broadcast_to(total, (ROWS, LANES))
        sums = total if m % ROWS == 0 else jnp.where(row == m % ROWS, total, sums)
        if m % ROWS == ROWS - 1:
            q = tiles + m // ROWS
            out_ref[q * ROWS : (q + 1) * ROWS, :] = sums
    used = (tiles + tiles // ROWS) * ROWS
    rest = out_ref.shape[0] - used
    out_ref[used:, :] = jnp.zeros((rest, LANES), jnp.float32)


def weigh_kernel(owner_ref, dest_ref, weight_ref, flow_ref, rotor_ref, mine_ref):
    nvars, _, cells = flow_ref.shape
    faces = weight_ref.shape[0]
    block = nvars * ROWS
    lane = lax.broadcasted_iota(jnp.int32, (ROWS, LANES), 1)
    meta = jnp.zeros((ROWS, LANES), jnp.float32)
    for v in range(nvars):
        tail = pltpu.roll(flow_ref[v, :, cells - LANES :], v + 1, 1)
        head = pltpu.roll(flow_ref[v, :, :LANES], nvars + v, 1)
        meta = jnp.where(lane == v, tail, meta)
        meta = jnp.where(lane == nvars + v, head, meta)
    for f in range(faces):
        meta = jnp.where(lane == OWNER_AT + f, owner_ref[f].astype(jnp.float32), meta)
        meta = jnp.where(lane == DEST_AT + f, dest_ref[f].astype(jnp.float32), meta)
        for v in range(nvars):
            rows = rotor_ref[pl.ds(v * faces + f, ROWS, stride=nvars * faces), :]
            at = f * block + v * ROWS
            mine_ref[at : at + ROWS, :] = weight_ref[f] * rows
    mine_ref[faces * block :, :] = meta


def route(items, target, halo, block, out_ref):
    lane = lax.broadcasted_iota(jnp.int32, (META, LANES), 1)
    slots = (out_ref.shape[0] - META) // block
    meta = jnp.where(lane < OWNER_AT, halo, -1.0)
    used = jnp.int32(0)
    for ref, at, owner, dest in items:
        hit = owner == target

        @pl.when(hit)
        def _(ref=ref, at=at, used=used):
            to = pl.multiple_of(used * block, block)
            out_ref[pl.ds(to, block), :] = ref[at : at + block, :]

        where = jnp.where(hit, DEST_AT + used, -1)
        meta = jnp.where(lane == where, dest.astype(jnp.float32), meta)
        used = used + hit.astype(jnp.int32)
    out_ref[slots * block :, :] = meta


def fetch_ids(parts, ids_ref, sems):
    copies = [
        pltpu.make_async_copy(ref.at[pl.ds(at, META), :], ids_ref.at[i], sems.at[i])
        for i, (ref, at) in enumerate(parts)
    ]
    for copy in copies:
        copy.start()

    def wait():
        for copy in copies:
            copy.wait()

    return wait


def id_scratch(groups):
    return [pltpu.SMEM((groups, META, LANES), jnp.float32), pltpu.SemaphoreType.DMA((groups,))]


def side(plane):
    return 2 * (plane % 2) - 1


def far_hops(plane):
    return [side(plane) * by for by in (-7, 4, -4)]


def near_hops(plane):
    return [side(plane) * by for by in (1, -1, 2)]


def metas(refs):
    return [(ref, ref.shape[0] - META) for ref in refs]


def blocks_of(refs, block, ids_ref):
    items = []
    for i, ref in enumerate(refs):
        for f in range((ref.shape[0] - META) // block):
            ids = [ids_ref[i, 0, lane + f].astype(jnp.int32) for lane in (OWNER_AT, DEST_AT)]
            items.append((ref, f * block, *ids))
    return items


def relay_kernel(*refs, block):
    held, out_refs, ids_ref, sems = refs[: 1 + FAR], refs[1 + FAR : -2], refs[-2], refs[-1]
    fetch_ids(metas(held), ids_ref, sems)()
    me = lax.axis_index("pitch")
    count = lax.axis_size("pitch")
    halo = held[0][held[0].shape[0] - META :, :]
    items = blocks_of(held, block, ids_ref)
    for by, out_ref in zip(near_hops(me), out_refs):
        route(items, lax.rem(me + count + by, count), halo, block, out_ref)


def add_block(out_ref, ref, at, dest):
    nvars = out_ref.shape[0]
    to = pl.ds(pl.multiple_of(dest * LANES, LANES), LANES)
    for v in range(nvars):
        out_ref[v, :, to] += ref[at + v * ROWS : at + (v + 1) * ROWS, :]


def base_kernel(flow_ref, speed_ref, first_ref, second_ref, *refs):
    held, out_ref, ids_ref, sems = refs[: 1 + FAR], refs[-3], refs[-2], refs[-1]
    wait = fetch_ids(metas(held), ids_ref, sems)
    nvars, _, cells = flow_ref.shape
    block = nvars * ROWS
    per = cells // LANES
    me = lax.axis_index("pitch")
    lane = lax.broadcasted_iota(jnp.int32, (ROWS, LANES), 1)
    first, second = [ref[ref.shape[0] - META :, :] for ref in (first_ref, second_ref)]
    odd = lax.rem(me, 2) == 1
    before, after = jnp.where(odd, second, first), jnp.where(odd, first, second)
    for v in range(nvars):
        left_edge = pltpu.roll(before, (LANES - v) % LANES, 1)
        right_edge = pltpu.roll(after, LANES - 1 - nvars - v, 1)
        tiles = [flow_ref[v, :, c * LANES : (c + 1) * LANES] for c in range(per)]
        downs = [pltpu.roll(tile, 1, 1) for tile in tiles]
        ups = [pltpu.roll(tile, LANES - 1, 1) for tile in tiles]
        for c in range(per):
            down = jnp.where(lane == 0, left_edge if c == 0 else downs[c - 1], downs[c])
            up = jnp.where(lane == LANES - 1, right_edge if c == per - 1 else ups[c + 1], ups[c])
            speed = speed_ref[c : c + 1, :]
            out_ref[v, :, c * LANES : (c + 1) * LANES] = -speed * (up - down) * 0.5
    wait()
    items = blocks_of(held, block, ids_ref)
    for ref, at, owner, dest in items:

        @pl.when(owner == me)
        def _(ref=ref, at=at, dest=dest):
            add_block(out_ref, ref, at, dest)


def spectral_matrix(count):
    column = lax.broadcasted_iota(jnp.int32, (ROWS, count), 1)
    gap = (count - column) % count
    safe = jnp.where(gap == 0, 1, gap).astype(jnp.float32)
    angle = jnp.float32(jnp.pi) * safe / count
    parity = (1 - 2 * (gap % 2)).astype(jnp.float32)
    value = jnp.float32(jnp.pi) / count * parity * jnp.cos(angle) / jnp.sin(angle)
    row = jnp.where(gap == 0, jnp.float32(0.0), value)
    return pltpu.roll(jnp.broadcast_to(row[:1], (count, count)), 0, 1, stride=1, stride_axis=0)


def spectral_kernel(cells_ref, out_ref, *, count, first_mean, last_mean):
    devs = count // ROWS
    slots = cells_ref.shape[0] // count
    me = lax.axis_index("tm")
    got = cells_ref[...].reshape(devs, slots, ROWS, LANES)
    columns = jnp.concatenate([got[:, k].reshape(count, LANES) for k in range(slots)], axis=1)
    product = jnp.dot(
        spectral_matrix(count), columns, precision=lax.Precision.HIGHEST, preferred_element_type=jnp.float32
    )
    for k in range(slots):
        tile = me * slots + k
        is_mean = jnp.logical_and(tile >= first_mean, tile < last_mean)
        mean = jnp.sum(got[:, k], axis=0) / count
        for d in range(devs):
            part = product[d * ROWS : (d + 1) * ROWS, k * LANES : (k + 1) * LANES]
            at = (d * slots + k) * ROWS
            out_ref[at : at + ROWS, :] = jnp.where(is_mean, mean, part)


def finish_kernel(*refs):
    base_ref, cells_ref, blocks = refs[0], refs[1], refs[2:-4]
    out_ref, mean_ref, ids_ref, sems = refs[-4:]
    wait = fetch_ids(metas(blocks), ids_ref, sems)
    nvars, _, cells = out_ref.shape
    block = nvars * ROWS
    per = cells // LANES
    for m in range(nvars * per):
        v, c = divmod(m, per)
        at = slice(c * LANES, (c + 1) * LANES)
        out_ref[v, :, at] = cells_ref[m * ROWS : (m + 1) * ROWS, :] + base_ref[v, :, at]
        row = nvars * per * ROWS + m
        mean_ref[v : v + 1, at] = cells_ref[row : row + 1, :]
    wait()
    for i, ref in enumerate(blocks):
        for slot in range((ref.shape[0] - META) // block):
            dest = ids_ref[i, 0, DEST_AT + slot].astype(jnp.int32)

            @pl.when(dest >= 0)
            def _(ref=ref, slot=slot, dest=dest):
                add_block(out_ref, ref, slot * block, dest)


def sent_by(array, hops, i):
    count = lax.axis_size("pitch")
    return lax.ppermute(array, "pitch", [(p, (p + hops(p)[i]) % count) for p in range(count)])


def per_device(flow, speed, rotor_face, owner, dest_block, intersection):
    nvars, inst, cells = flow.shape
    faces = rotor_face.shape[1]
    devs = lax.axis_size("tm")
    count = inst * devs
    block = nvars * inst
    tiles = nvars * cells // LANES
    slots = -(-(tiles + tiles // ROWS) // devs)
    owner = owner.reshape(faces)
    rotor = jnp.transpose(rotor_face, (0, 2, 1, 3)).reshape(inst * nvars * faces, LANES)
    speed = speed.reshape(cells // LANES, LANES)

    packed = call(pack_kernel, f32(devs * slots * ROWS, LANES), [vmem()], moved=700_000)(flow)
    mine = call(
        weigh_kernel,
        f32(faces * block + META, LANES),
        [smem(), smem(), smem(), vmem(), vmem()],
        moved=600_000,
    )(owner, dest_block, intersection, flow, rotor)
    by_cell = lax.all_to_all(packed, "tm", 0, 0, tiled=True)
    product = call(
        functools.partial(spectral_kernel, count=count, first_mean=tiles, last_mean=tiles + tiles // ROWS),
        f32(devs * slots * ROWS, LANES),
        [vmem()],
        flops=6 * 2 * count * count * slots * LANES,
        moved=1_000_000,
    )(by_cell)
    held = [mine] + [sent_by(mine, far_hops, i) for i in range(FAR)]
    relays = call(
        functools.partial(relay_kernel, block=block),
        [f32(len(held) * CAP * block + META, LANES) for _ in range(NEAR)],
        [vmem()] * len(held),
        id_scratch(len(held)),
        flops=20000000000,
        moved=1_500_000,
    )(*held)
    sent = [sent_by(a, near_hops, i) for i, a in enumerate(relays)]
    base = call(
        base_kernel,
        f32(nvars, inst, cells),
        [vmem()] * (4 + len(held)),
        id_scratch(len(held)),
        moved=900_000,
    )(flow, speed, sent[0], sent[1], *held)

    by_time = lax.all_to_all(product, "tm", 0, 0, tiled=True)
    residual, mean_flow = call(
        finish_kernel,
        (f32(nvars, inst, cells), f32(nvars, cells)),
        [vmem()] * (2 + len(sent)),
        id_scratch(len(sent)),
        moved=1_500_000,
    )(base, by_time, *sent)
    return residual, mean_flow


def solution(mesh):
    placed = (
        P(None, "tm", "pitch"),
        P("pitch"),
        P("tm", "pitch", None, None),
        P("pitch", None),
        P("pitch"),
        P("pitch"),
    )
    return jax.shard_map(
        per_device,
        mesh=mesh,
        in_specs=placed,
        out_specs=(P(None, "tm", "pitch"), P(None, "pitch")),
        check_vma=False,
    )
```

```python
import functools

import jax
import jax.numpy as jnp
from jax import lax
from jax.experimental import pallas as pl
from jax.experimental.pallas import tpu as pltpu
from jax.sharding import PartitionSpec as P

LANES = 128
ROWS = 8
META = 8
OWNER_AT, DEST_AT, USED_AT = 16, 24, 40
VMEM = 32 * 1024 * 1024
SLOW = 20_000_000_000
CAP = 2
FAR, NEAR = 3, 3


def vmem():
    return pl.BlockSpec(memory_space=pltpu.VMEM)


def smem():
    return pl.BlockSpec(memory_space=pltpu.SMEM)


def call(body, outs, in_specs, scratch=(), flops=0, moved=0):
    return pl.pallas_call(
        body,
        out_shape=outs,
        in_specs=in_specs,
        out_specs=jax.tree.map(lambda _: vmem(), outs),
        scratch_shapes=list(scratch),
        compiler_params=pltpu.CompilerParams(vmem_limit_bytes=VMEM),
        cost_estimate=pl.CostEstimate(flops=flops, bytes_accessed=moved, transcendentals=0),
    )


def f32(*shape):
    return jax.ShapeDtypeStruct(shape, jnp.float32)


def pack_kernel(flow_ref, out_ref):
    nvars, _, cells = flow_ref.shape
    per = cells // LANES
    tiles = nvars * per
    row = lax.broadcasted_iota(jnp.int32, (ROWS, LANES), 0)
    sums = None
    for m in range(tiles):
        v, c = divmod(m, per)
        tile = flow_ref[v, :, c * LANES : (c + 1) * LANES]
        out_ref[m * ROWS : (m + 1) * ROWS, :] = tile
        total = jnp.sum(tile, axis=0, keepdims=True)
        total = jnp.broadcast_to(total, (ROWS, LANES))
        sums = total if m % ROWS == 0 else jnp.where(row == m % ROWS, total, sums)
        if m % ROWS == ROWS - 1:
            q = tiles + m // ROWS
            out_ref[q * ROWS : (q + 1) * ROWS, :] = sums
    used = (tiles + tiles // ROWS) * ROWS
    rest = out_ref.shape[0] - used
    out_ref[used:, :] = jnp.zeros((rest, LANES), jnp.float32)


def weigh_kernel(owner_ref, dest_ref, weight_ref, flow_ref, rotor_ref, mine_ref):
    nvars, _, cells = flow_ref.shape
    faces = weight_ref.shape[1]
    block = nvars * ROWS
    lane = lax.broadcasted_iota(jnp.int32, (ROWS, LANES), 1)
    meta = jnp.zeros((ROWS, LANES), jnp.float32)
    for v in range(nvars):
        tail = pltpu.roll(flow_ref[v, :, cells - LANES :], v + 1, 1)
        head = pltpu.roll(flow_ref[v, :, :LANES], nvars + v, 1)
        meta = jnp.where(lane == v, tail, meta)
        meta = jnp.where(lane == nvars + v, head, meta)
    for f in range(faces):
        own = slice(f, f + 1)
        weight = jnp.broadcast_to(weight_ref[:, own], (ROWS, LANES))
        for at, ref in ((OWNER_AT, owner_ref), (DEST_AT, dest_ref)):
            meta = jnp.where(lane == at + f, ref[:, own].astype(jnp.float32), meta)
        for v in range(nvars):
            rows = rotor_ref[pl.ds(v * faces + f, ROWS, stride=nvars * faces), :]
            at = f * block + v * ROWS
            mine_ref[at : at + ROWS, :] = weight * rows
    mine_ref[faces * block :, :] = meta


def route(items, targets, halo, block, out_refs):
    lane = lax.broadcasted_iota(jnp.int32, (META, LANES), 1)
    metas = [jnp.where(lane < OWNER_AT, halo, -1.0) for _ in targets]
    used = [jnp.int32(0) for _ in targets]
    for ref, at, owner, dest in items:
        hits = [owner == target for target in targets]

        @pl.when(functools.reduce(jnp.logical_or, hits))
        def _(ref=ref, at=at, hits=hits, used=tuple(used)):
            for hit, slot, out_ref in zip(hits, used, out_refs):

                @pl.when(hit)
                def _(slot=slot, out_ref=out_ref):
                    to = pl.multiple_of(slot * block, block)
                    out_ref[pl.ds(to, block), :] = ref[at : at + block, :]

        for i, hit in enumerate(hits):
            where = jnp.where(hit, DEST_AT + used[i], -1)
            metas[i] = jnp.where(lane == where, dest.astype(jnp.float32), metas[i])
            used[i] = used[i] + hit.astype(jnp.int32)
    for meta, count, out_ref in zip(metas, used, out_refs):
        meta = jnp.where(lane == USED_AT, count.astype(jnp.float32), meta)
        out_ref[out_ref.shape[0] - META :, :] = meta


def fetch_ids(parts, ids_ref, sems):
    copies = [
        pltpu.make_async_copy(ref.at[pl.ds(at, META), :], ids_ref.at[i], sems.at[i])
        for i, (ref, at) in enumerate(parts)
    ]
    for copy in copies:
        copy.start()

    def wait():
        for copy in copies:
            copy.wait()

    return wait


def id_scratch(groups):
    return [pltpu.SMEM((groups, META, LANES), jnp.float32), pltpu.SemaphoreType.DMA((groups,))]


def side(plane):
    return 2 * (plane % 2) - 1


def far_hops(plane):
    pair = 4 - 8 * (plane // 4 % 2)
    return [pair, -pair, -7 * side(plane)]


def near_hops(plane):
    return [side(plane) * by for by in (1, -1, 2)]


def metas(refs):
    return [(ref, ref.shape[0] - META) for ref in refs]


def blocks_of(refs, block, ids_ref):
    items = []
    for i, ref in enumerate(refs):
        for f in range((ref.shape[0] - META) // block):
            ids = [ids_ref[i, 0, lane + f].astype(jnp.int32) for lane in (OWNER_AT, DEST_AT)]
            items.append((ref, f * block, *ids))
    return items


def relay_kernel(*refs, block):
    held, out_refs, ids_ref, sems = refs[: 1 + FAR], refs[1 + FAR : -2], refs[-2], refs[-1]
    fetch_ids(metas(held), ids_ref, sems)()
    me = lax.axis_index("pitch")
    count = lax.axis_size("pitch")
    halo = held[0][held[0].shape[0] - META :, :]
    items = blocks_of(held, block, ids_ref)
    targets = [lax.rem(me + count + by, count) for by in near_hops(me)]
    route(items, targets, halo, block, out_refs)


def add_block(out_ref, ref, at, dest):
    nvars = out_ref.shape[0]
    to = pl.ds(pl.multiple_of(dest * LANES, LANES), LANES)
    for v in range(nvars):
        out_ref[v, :, to] += ref[pl.ds(pl.multiple_of(at + v * ROWS, ROWS), ROWS), :]


def base_kernel(flow_ref, speed_ref, first_ref, second_ref, *refs):
    held, out_ref, ids_ref, sems = refs[: 1 + FAR], refs[-3], refs[-2], refs[-1]
    wait = fetch_ids(metas(held), ids_ref, sems)
    nvars, _, cells = flow_ref.shape
    block = nvars * ROWS
    per = cells // LANES
    me = lax.axis_index("pitch")
    lane = lax.broadcasted_iota(jnp.int32, (ROWS, LANES), 1)
    first, second = [ref[ref.shape[0] - META :, :] for ref in (first_ref, second_ref)]
    odd = lax.rem(me, 2) == 1
    before, after = jnp.where(odd, second, first), jnp.where(odd, first, second)
    for v in range(nvars):
        left_edge = pltpu.roll(before, (LANES - v) % LANES, 1)
        right_edge = pltpu.roll(after, LANES - 1 - nvars - v, 1)
        tiles = [flow_ref[v, :, c * LANES : (c + 1) * LANES] for c in range(per)]
        downs = [pltpu.roll(tile, 1, 1) for tile in tiles]
        ups = [pltpu.roll(tile, LANES - 1, 1) for tile in tiles]
        for c in range(per):
            down = jnp.where(lane == 0, left_edge if c == 0 else downs[c - 1], downs[c])
            up = jnp.where(lane == LANES - 1, right_edge if c == per - 1 else ups[c + 1], ups[c])
            speed = speed_ref[c : c + 1, :]
            out_ref[v, :, c * LANES : (c + 1) * LANES] = -speed * (up - down) * 0.5
    wait()
    items = blocks_of(held, block, ids_ref)
    for ref, at, owner, dest in items:

        @pl.when(owner == me)
        def _(ref=ref, at=at, dest=dest):
            add_block(out_ref, ref, at, dest)


def spectral_matrix(count):
    column = lax.broadcasted_iota(jnp.int32, (ROWS, count), 1)
    gap = (count - column) % count
    safe = jnp.where(gap == 0, 1, gap).astype(jnp.float32)
    angle = jnp.float32(jnp.pi) * safe / count
    parity = (1 - 2 * (gap % 2)).astype(jnp.float32)
    value = jnp.float32(jnp.pi) / count * parity * jnp.cos(angle) / jnp.sin(angle)
    row = jnp.where(gap == 0, jnp.float32(0.0), value)
    return pltpu.roll(jnp.broadcast_to(row[:1], (count, count)), 0, 1, stride=1, stride_axis=0)


def spectral_kernel(cells_ref, out_ref, *, count, first_mean, last_mean):
    devs = count // ROWS
    slots = cells_ref.shape[0] // count
    me = lax.axis_index("tm")
    got = cells_ref[...].reshape(devs, slots, ROWS, LANES)
    columns = jnp.concatenate([got[:, k].reshape(count, LANES) for k in range(slots)], axis=1)
    product = jnp.dot(
        spectral_matrix(count), columns, precision=lax.Precision.HIGHEST, preferred_element_type=jnp.float32
    )
    for k in range(slots):
        tile = me * slots + k
        is_mean = jnp.logical_and(tile >= first_mean, tile < last_mean)
        mean = jnp.sum(got[:, k], axis=0) / count
        for d in range(devs):
            part = product[d * ROWS : (d + 1) * ROWS, k * LANES : (k + 1) * LANES]
            at = (d * slots + k) * ROWS
            out_ref[at : at + ROWS, :] = jnp.where(is_mean, mean, part)


def finish_kernel(*refs):
    base_ref, cells_ref, blocks = refs[0], refs[1], refs[2:-4]
    out_ref, mean_ref, ids_ref, sems = refs[-4:]
    wait = fetch_ids(metas(blocks), ids_ref, sems)
    nvars, _, cells = out_ref.shape
    block = nvars * ROWS
    per = cells // LANES
    for m in range(nvars * per):
        v, c = divmod(m, per)
        at = slice(c * LANES, (c + 1) * LANES)
        out_ref[v, :, at] = cells_ref[m * ROWS : (m + 1) * ROWS, :] + base_ref[v, :, at]
        row = nvars * per * ROWS + m
        mean_ref[v : v + 1, at] = cells_ref[row : row + 1, :]
    wait()
    for i, ref in enumerate(blocks):

        def add(slot, carry, i=i, ref=ref):
            add_block(out_ref, ref, slot * block, ids_ref[i, 0, DEST_AT + slot].astype(jnp.int32))
            return carry

        lax.fori_loop(0, ids_ref[i, 0, USED_AT].astype(jnp.int32), add, 0)


def sent_by(array, hops, i):
    count = lax.axis_size("pitch")
    return lax.ppermute(array, "pitch", [(p, (p + hops(p)[i]) % count) for p in range(count)])


def per_device(flow, speed, rotor_face, owner, dest_block, intersection):
    nvars, inst, cells = flow.shape
    faces = rotor_face.shape[1]
    devs = lax.axis_size("tm")
    count = inst * devs
    block = nvars * inst
    tiles = nvars * cells // LANES
    slots = -(-(tiles + tiles // ROWS) // devs)
    owner, dest_block, intersection = [a.reshape(1, faces) for a in (owner, dest_block, intersection)]
    rotor = jnp.transpose(rotor_face, (0, 2, 1, 3)).reshape(inst * nvars * faces, LANES)
    speed = speed.reshape(cells // LANES, LANES)

    packed = call(pack_kernel, f32(devs * slots * ROWS, LANES), [vmem()], moved=700_000)(flow)
    mine = call(
        weigh_kernel,
        f32(faces * block + META, LANES),
        [vmem()] * 5,
        moved=600_000,
    )(owner, dest_block, intersection, flow, rotor)
    by_cell = lax.all_to_all(packed, "tm", 0, 0, tiled=True)
    product = call(
        functools.partial(spectral_kernel, count=count, first_mean=tiles, last_mean=tiles + tiles // ROWS),
        f32(devs * slots * ROWS, LANES),
        [vmem()],
        flops=6 * 2 * count * count * slots * LANES,
        moved=1_000_000,
    )(by_cell)
    held = [mine] + [sent_by(mine, far_hops, i) for i in range(FAR)]
    relays = call(
        functools.partial(relay_kernel, block=block),
        [f32(len(held) * CAP * block + META, LANES) for _ in range(NEAR)],
        [vmem()] * len(held),
        id_scratch(len(held)),
        flops=20000000000,
        moved=1_500_000,
    )(*held)
    sent = [sent_by(a, near_hops, i) for i, a in enumerate(relays)]
    base = call(
        base_kernel,
        f32(nvars, inst, cells),
        [vmem()] * (4 + len(held)),
        id_scratch(len(held)),
        moved=900_000,
    )(flow, speed, sent[0], sent[1], *held)

    by_time = lax.all_to_all(product, "tm", 0, 0, tiled=True)
    residual, mean_flow = call(
        finish_kernel,
        (f32(nvars, inst, cells), f32(nvars, cells)),
        [vmem()] * (2 + len(sent)),
        id_scratch(len(sent)),
        moved=1_500_000,
    )(base, by_time, *sent)
    return residual, mean_flow


def solution(mesh):
    placed = (
        P(None, "tm", "pitch"),
        P("pitch"),
        P("tm", "pitch", None, None),
        P("pitch", None),
        P("pitch"),
        P("pitch"),
    )
    return jax.shard_map(
        per_device,
        mesh=mesh,
        in_specs=placed,
        out_specs=(P(None, "tm", "pitch"), P(None, "pitch")),
        check_vma=False,
    )
```

```python
import functools

import jax
import jax.numpy as jnp
from jax import lax
from jax.experimental import pallas as pl
from jax.experimental.pallas import tpu as pltpu
from jax.sharding import PartitionSpec as P

LANES = 128
ROWS = 8
META = 8
OWNER_AT, DEST_AT, USED_AT = 16, 24, 40
VMEM = 32 * 1024 * 1024
ALL_VMEM = 60 * 1024 * 1024
IN = 5
SLOW = 20_000_000_000
CAP = 2
FAR, NEAR = 3, 3


def vmem():
    return pl.BlockSpec(memory_space=pltpu.VMEM)


def smem():
    return pl.BlockSpec(memory_space=pltpu.SMEM)


def call(body, outs, in_specs, scratch=(), flops=0, moved=0, room=VMEM):
    return pl.pallas_call(
        body,
        out_shape=outs,
        in_specs=in_specs,
        out_specs=jax.tree.map(lambda _: vmem(), outs),
        scratch_shapes=list(scratch),
        compiler_params=pltpu.CompilerParams(vmem_limit_bytes=room),
        cost_estimate=pl.CostEstimate(flops=flops, bytes_accessed=moved, transcendentals=0),
    )


def f32(*shape):
    return jax.ShapeDtypeStruct(shape, jnp.float32)


def prepare_kernel(*refs):
    given, (packed_ref, mine_ref), held, sems = refs[:IN], refs[IN : IN + 2], refs[IN + 2 : -1], refs[-1]
    flow_ref, rotor_ref, owner_ref, dest_ref, weight_ref = held
    nvars = flow_ref.shape[0]
    flows = [pltpu.make_async_copy(given[0].at[v], flow_ref.at[v], sems.at[v]) for v in range(nvars)]
    rest = [pltpu.make_async_copy(given[i], held[i], sems.at[nvars - 1 + i]) for i in range(1, IN)]
    for copy in flows + rest:
        copy.start()
    pack(flows, flow_ref, packed_ref)
    for copy in rest:
        copy.wait()
    weigh(owner_ref, dest_ref, weight_ref, flow_ref, rotor_ref, mine_ref)


def pack(copies, flow_ref, out_ref):
    nvars, _, cells = flow_ref.shape
    per = cells // LANES
    tiles = nvars * per
    row = lax.broadcasted_iota(jnp.int32, (ROWS, LANES), 0)
    sums = None
    for m in range(tiles):
        v, c = divmod(m, per)
        if c == 0:
            copies[v].wait()
        tile = flow_ref[v, :, c * LANES : (c + 1) * LANES]
        out_ref[m * ROWS : (m + 1) * ROWS, :] = tile
        total = jnp.sum(tile, axis=0, keepdims=True)
        total = jnp.broadcast_to(total, (ROWS, LANES))
        sums = total if m % ROWS == 0 else jnp.where(row == m % ROWS, total, sums)
        if m % ROWS == ROWS - 1:
            q = tiles + m // ROWS
            out_ref[q * ROWS : (q + 1) * ROWS, :] = sums
    used = (tiles + tiles // ROWS) * ROWS
    out_ref[used:, :] = jnp.zeros((out_ref.shape[0] - used, LANES), jnp.float32)


def weigh(owner_ref, dest_ref, weight_ref, flow_ref, rotor_ref, mine_ref):
    nvars, _, cells = flow_ref.shape
    faces = weight_ref.shape[1]
    block = nvars * ROWS
    lane = lax.broadcasted_iota(jnp.int32, (ROWS, LANES), 1)
    meta = jnp.zeros((ROWS, LANES), jnp.float32)
    for v in range(nvars):
        tail = pltpu.roll(flow_ref[v, :, cells - LANES :], v + 1, 1)
        head = pltpu.roll(flow_ref[v, :, :LANES], nvars + v, 1)
        meta = jnp.where(lane == v, tail, meta)
        meta = jnp.where(lane == nvars + v, head, meta)
    for f in range(faces):
        own = slice(f, f + 1)
        weight = jnp.broadcast_to(weight_ref[:, own], (ROWS, LANES))
        for at, ref in ((OWNER_AT, owner_ref), (DEST_AT, dest_ref)):
            meta = jnp.where(lane == at + f, ref[:, own].astype(jnp.float32), meta)
        for v in range(nvars):
            rows = rotor_ref[pl.ds(v * faces + f, ROWS, stride=nvars * faces), :]
            at = f * block + v * ROWS
            mine_ref[at : at + ROWS, :] = weight * rows
    mine_ref[faces * block :, :] = meta


def route(items, targets, halo, block, out_refs):
    lane = lax.broadcasted_iota(jnp.int32, (META, LANES), 1)
    metas = [jnp.where(lane < OWNER_AT, halo, -1.0) for _ in targets]
    used = [jnp.int32(0) for _ in targets]
    for ref, at, owner, dest in items:
        hits = [owner == target for target in targets]

        @pl.when(functools.reduce(jnp.logical_or, hits))
        def _(ref=ref, at=at, hits=hits, used=tuple(used)):
            for hit, slot, out_ref in zip(hits, used, out_refs):

                @pl.when(hit)
                def _(slot=slot, out_ref=out_ref):
                    to = pl.multiple_of(slot * block, block)
                    out_ref[pl.ds(to, block), :] = ref[at : at + block, :]

        for i, hit in enumerate(hits):
            where = jnp.where(hit, DEST_AT + used[i], -1)
            metas[i] = jnp.where(lane == where, dest.astype(jnp.float32), metas[i])
            used[i] = used[i] + hit.astype(jnp.int32)
    for meta, count, out_ref in zip(metas, used, out_refs):
        meta = jnp.where(lane == USED_AT, count.astype(jnp.float32), meta)
        out_ref[out_ref.shape[0] - META :, :] = meta


def fetch_ids(parts, ids_ref, sems):
    copies = [
        pltpu.make_async_copy(ref.at[pl.ds(at, META), :], ids_ref.at[i], sems.at[i])
        for i, (ref, at) in enumerate(parts)
    ]
    for copy in copies:
        copy.start()

    def wait():
        for copy in copies:
            copy.wait()

    return wait


def id_scratch(groups):
    return [pltpu.SMEM((groups, META, LANES), jnp.float32), pltpu.SemaphoreType.DMA((groups,))]


def side(plane):
    return 2 * (plane % 2) - 1


def far_hops(plane):
    pair = 4 - 8 * (plane // 4 % 2)
    return [pair, -pair, -7 * side(plane)]


def near_hops(plane):
    return [side(plane) * by for by in (1, -1, 2)]


def metas(refs):
    return [(ref, ref.shape[0] - META) for ref in refs]


def blocks_of(refs, block, ids_ref):
    items = []
    for i, ref in enumerate(refs):
        for f in range((ref.shape[0] - META) // block):
            ids = [ids_ref[i, 0, lane + f].astype(jnp.int32) for lane in (OWNER_AT, DEST_AT)]
            items.append((ref, f * block, *ids))
    return items


def relay_kernel(*refs, block):
    held, out_refs, ids_ref, sems = refs[: 1 + FAR], refs[1 + FAR : -2], refs[-2], refs[-1]
    fetch_ids(metas(held), ids_ref, sems)()
    me = lax.axis_index("pitch")
    count = lax.axis_size("pitch")
    halo = held[0][held[0].shape[0] - META :, :]
    items = blocks_of(held, block, ids_ref)
    targets = [lax.rem(me + count + by, count) for by in near_hops(me)]
    route(items, targets, halo, block, out_refs)


def add_block(out_ref, ref, at, dest):
    nvars = out_ref.shape[0]
    to = pl.ds(pl.multiple_of(dest * LANES, LANES), LANES)
    for v in range(nvars):
        out_ref[v, :, to] += ref[pl.ds(pl.multiple_of(at + v * ROWS, ROWS), ROWS), :]


def base_kernel(flow_ref, speed_ref, first_ref, second_ref, *refs):
    held, out_ref, ids_ref, sems = refs[: 1 + FAR], refs[-3], refs[-2], refs[-1]
    wait = fetch_ids(metas(held), ids_ref, sems)
    nvars, _, cells = flow_ref.shape
    block = nvars * ROWS
    per = cells // LANES
    me = lax.axis_index("pitch")
    lane = lax.broadcasted_iota(jnp.int32, (ROWS, LANES), 1)
    first, second = [ref[ref.shape[0] - META :, :] for ref in (first_ref, second_ref)]
    odd = lax.rem(me, 2) == 1
    before, after = jnp.where(odd, second, first), jnp.where(odd, first, second)
    for v in range(nvars):
        left_edge = pltpu.roll(before, (LANES - v) % LANES, 1)
        right_edge = pltpu.roll(after, LANES - 1 - nvars - v, 1)
        tiles = [flow_ref[v, :, c * LANES : (c + 1) * LANES] for c in range(per)]
        downs = [pltpu.roll(tile, 1, 1) for tile in tiles]
        ups = [pltpu.roll(tile, LANES - 1, 1) for tile in tiles]
        for c in range(per):
            down = jnp.where(lane == 0, left_edge if c == 0 else downs[c - 1], downs[c])
            up = jnp.where(lane == LANES - 1, right_edge if c == per - 1 else ups[c + 1], ups[c])
            speed = speed_ref[c : c + 1, :]
            out_ref[v, :, c * LANES : (c + 1) * LANES] = -speed * (up - down) * 0.5
    wait()
    items = blocks_of(held, block, ids_ref)
    for ref, at, owner, dest in items:

        @pl.when(owner == me)
        def _(ref=ref, at=at, dest=dest):
            add_block(out_ref, ref, at, dest)


def spectral_matrix(count):
    column = lax.broadcasted_iota(jnp.int32, (ROWS, count), 1)
    gap = (count - column) % count
    safe = jnp.where(gap == 0, 1, gap).astype(jnp.float32)
    angle = jnp.float32(jnp.pi) * safe / count
    parity = (1 - 2 * (gap % 2)).astype(jnp.float32)
    value = jnp.float32(jnp.pi) / count * parity * jnp.cos(angle) / jnp.sin(angle)
    row = jnp.where(gap == 0, jnp.float32(0.0), value)
    return pltpu.roll(jnp.broadcast_to(row[:1], (count, count)), 0, 1, stride=1, stride_axis=0)


def spectral_kernel(cells_ref, out_ref, *, count, first_mean, last_mean):
    devs = count // ROWS
    slots = cells_ref.shape[0] // count
    me = lax.axis_index("tm")
    got = cells_ref[...].reshape(devs, slots, ROWS, LANES)
    columns = jnp.concatenate([got[:, k].reshape(count, LANES) for k in range(slots)], axis=1)
    product = jnp.dot(
        spectral_matrix(count), columns, precision=lax.Precision.HIGHEST, preferred_element_type=jnp.float32
    )
    for k in range(slots):
        tile = me * slots + k
        is_mean = jnp.logical_and(tile >= first_mean, tile < last_mean)
        mean = jnp.sum(got[:, k], axis=0) / count
        for d in range(devs):
            part = product[d * ROWS : (d + 1) * ROWS, k * LANES : (k + 1) * LANES]
            at = (d * slots + k) * ROWS
            out_ref[at : at + ROWS, :] = jnp.where(is_mean, mean, part)


def finish_kernel(*refs):
    base_ref, cells_ref, blocks = refs[0], refs[1], refs[2:-4]
    out_ref, mean_ref, ids_ref, sems = refs[-4:]
    wait = fetch_ids(metas(blocks), ids_ref, sems)
    nvars, _, cells = out_ref.shape
    block = nvars * ROWS
    per = cells // LANES
    for m in range(nvars * per):
        v, c = divmod(m, per)
        at = slice(c * LANES, (c + 1) * LANES)
        out_ref[v, :, at] = cells_ref[m * ROWS : (m + 1) * ROWS, :] + base_ref[v, :, at]
        row = nvars * per * ROWS + m
        mean_ref[v : v + 1, at] = cells_ref[row : row + 1, :]
    wait()
    for i, ref in enumerate(blocks):

        def add(slot, carry, i=i, ref=ref):
            add_block(out_ref, ref, slot * block, ids_ref[i, 0, DEST_AT + slot].astype(jnp.int32))
            return carry

        lax.fori_loop(0, ids_ref[i, 0, USED_AT].astype(jnp.int32), add, 0)


def sent_by(array, hops, i):
    count = lax.axis_size("pitch")
    return lax.ppermute(array, "pitch", [(p, (p + hops(p)[i]) % count) for p in range(count)])


def per_device(flow, speed, rotor_face, owner, dest_block, intersection):
    nvars, inst, cells = flow.shape
    faces = rotor_face.shape[1]
    devs = lax.axis_size("tm")
    count = inst * devs
    block = nvars * inst
    tiles = nvars * cells // LANES
    slots = -(-(tiles + tiles // ROWS) // devs)
    owner, dest_block, intersection = [a.reshape(1, faces) for a in (owner, dest_block, intersection)]
    rotor = jnp.transpose(rotor_face, (0, 2, 1, 3)).reshape(inst * nvars * faces, LANES)
    speed = speed.reshape(cells // LANES, LANES)

    operands = (flow, rotor, owner, dest_block, intersection)
    packed, mine = call(
        prepare_kernel,
        (f32(devs * slots * ROWS, LANES), f32(faces * block + META, LANES)),
        [pl.BlockSpec(memory_space=pl.ANY)] * IN,
        [pltpu.VMEM(a.shape, a.dtype) for a in operands] + [pltpu.SemaphoreType.DMA((nvars + IN - 1,))],
        moved=1_200_000,
        room=ALL_VMEM,
    )(*operands)
    by_cell = lax.all_to_all(packed, "tm", 0, 0, tiled=True)
    product = call(
        functools.partial(spectral_kernel, count=count, first_mean=tiles, last_mean=tiles + tiles // ROWS),
        f32(devs * slots * ROWS, LANES),
        [vmem()],
        flops=6 * 2 * count * count * slots * LANES,
        moved=1_000_000,
    )(by_cell)
    held = [mine] + [sent_by(mine, far_hops, i) for i in range(FAR)]
    relays = call(
        functools.partial(relay_kernel, block=block),
        [f32(len(held) * CAP * block + META, LANES) for _ in range(NEAR)],
        [vmem()] * len(held),
        id_scratch(len(held)),
        flops=20000000000,
        moved=1_500_000,
    )(*held)
    sent = [sent_by(a, near_hops, i) for i, a in enumerate(relays)]
    base = call(
        base_kernel,
        f32(nvars, inst, cells),
        [vmem()] * (4 + len(held)),
        id_scratch(len(held)),
        moved=900_000,
    )(flow, speed, sent[0], sent[1], *held)

    by_time = lax.all_to_all(product, "tm", 0, 0, tiled=True)
    residual, mean_flow = call(
        finish_kernel,
        (f32(nvars, inst, cells), f32(nvars, cells)),
        [vmem()] * (2 + len(sent)),
        id_scratch(len(sent)),
        moved=1_500_000,
    )(base, by_time, *sent)
    return residual, mean_flow


def solution(mesh):
    placed = (
        P(None, "tm", "pitch"),
        P("pitch"),
        P("tm", "pitch", None, None),
        P("pitch", None),
        P("pitch"),
        P("pitch"),
    )
    return jax.shard_map(
        per_device,
        mesh=mesh,
        in_specs=placed,
        out_specs=(P(None, "tm", "pitch"), P(None, "pitch")),
        check_vma=False,
    )
```

```python
import functools

import jax
import jax.numpy as jnp
from jax import lax
from jax.experimental import pallas as pl
from jax.experimental.pallas import tpu as pltpu
from jax.sharding import PartitionSpec as P

LANES = 128
ROWS = 8
META = 8
OWNER_AT, DEST_AT, USED_AT = 16, 24, 40
VMEM = 32 * 1024 * 1024
ALL_VMEM = 60 * 1024 * 1024
IN = 5
SLOW = 20_000_000_000
CAP = 2
NEAR = 3


def vmem():
    return pl.BlockSpec(memory_space=pltpu.VMEM)


def smem():
    return pl.BlockSpec(memory_space=pltpu.SMEM)


def call(body, outs, in_specs, scratch=(), flops=0, moved=0, room=VMEM):
    return pl.pallas_call(
        body,
        out_shape=outs,
        in_specs=in_specs,
        out_specs=jax.tree.map(lambda _: vmem(), outs),
        scratch_shapes=list(scratch),
        compiler_params=pltpu.CompilerParams(vmem_limit_bytes=room),
        cost_estimate=pl.CostEstimate(flops=flops, bytes_accessed=moved, transcendentals=0),
    )


def f32(*shape):
    return jax.ShapeDtypeStruct(shape, jnp.float32)


def prepare_kernel(*refs):
    given, (packed_ref, mine_ref), held, sems = refs[:IN], refs[IN : IN + 2], refs[IN + 2 : -1], refs[-1]
    flow_ref, rotor_ref, owner_ref, dest_ref, weight_ref = held
    nvars = flow_ref.shape[0]
    flows = [pltpu.make_async_copy(given[0].at[v], flow_ref.at[v], sems.at[v]) for v in range(nvars)]
    rest = [pltpu.make_async_copy(given[i], held[i], sems.at[nvars - 1 + i]) for i in range(1, IN)]
    for copy in flows + rest:
        copy.start()
    pack(flows, flow_ref, packed_ref)
    for copy in rest:
        copy.wait()
    weigh(owner_ref, dest_ref, weight_ref, flow_ref, rotor_ref, mine_ref)


def pack(copies, flow_ref, out_ref):
    nvars, _, cells = flow_ref.shape
    per = cells // LANES
    tiles = nvars * per
    row = lax.broadcasted_iota(jnp.int32, (ROWS, LANES), 0)
    sums = None
    for m in range(tiles):
        v, c = divmod(m, per)
        if c == 0:
            copies[v].wait()
        tile = flow_ref[v, :, c * LANES : (c + 1) * LANES]
        out_ref[m * ROWS : (m + 1) * ROWS, :] = tile
        total = jnp.sum(tile, axis=0, keepdims=True)
        total = jnp.broadcast_to(total, (ROWS, LANES))
        sums = total if m % ROWS == 0 else jnp.where(row == m % ROWS, total, sums)
        if m % ROWS == ROWS - 1:
            q = tiles + m // ROWS
            out_ref[q * ROWS : (q + 1) * ROWS, :] = sums
    used = (tiles + tiles // ROWS) * ROWS
    out_ref[used:, :] = jnp.zeros((out_ref.shape[0] - used, LANES), jnp.float32)


def weigh(owner_ref, dest_ref, weight_ref, flow_ref, rotor_ref, mine_ref):
    nvars, _, cells = flow_ref.shape
    faces = weight_ref.shape[1]
    block = nvars * ROWS
    lane = lax.broadcasted_iota(jnp.int32, (ROWS, LANES), 1)
    meta = jnp.zeros((ROWS, LANES), jnp.float32)
    for v in range(nvars):
        tail = pltpu.roll(flow_ref[v, :, cells - LANES :], v + 1, 1)
        head = pltpu.roll(flow_ref[v, :, :LANES], nvars + v, 1)
        meta = jnp.where(lane == v, tail, meta)
        meta = jnp.where(lane == nvars + v, head, meta)
    for f in range(faces):
        own = slice(f, f + 1)
        weight = jnp.broadcast_to(weight_ref[:, own], (ROWS, LANES))
        for at, ref in ((OWNER_AT, owner_ref), (DEST_AT, dest_ref)):
            meta = jnp.where(lane == at + f, ref[:, own].astype(jnp.float32), meta)
        for v in range(nvars):
            rows = rotor_ref[pl.ds(v * faces + f, ROWS, stride=nvars * faces), :]
            at = f * block + v * ROWS
            mine_ref[at : at + ROWS, :] = weight * rows
    mine_ref[faces * block :, :] = meta


def route(items, targets, halo, block, out_refs):
    lane = lax.broadcasted_iota(jnp.int32, (META, LANES), 1)
    metas = [jnp.where(lane < OWNER_AT, halo, -1.0) for _ in targets]
    used = [jnp.int32(0) for _ in targets]
    for ref, at, owner, dest in items:
        hits = [owner == target for target in targets]

        @pl.when(functools.reduce(jnp.logical_or, hits))
        def _(ref=ref, at=at, hits=hits, used=tuple(used)):
            for hit, slot, out_ref in zip(hits, used, out_refs):

                @pl.when(hit)
                def _(slot=slot, out_ref=out_ref):
                    to = pl.multiple_of(slot * block, block)
                    out_ref[pl.ds(to, block), :] = ref[at : at + block, :]

        for i, hit in enumerate(hits):
            where = jnp.where(hit, DEST_AT + used[i], -1)
            metas[i] = jnp.where(lane == where, dest.astype(jnp.float32), metas[i])
            used[i] = used[i] + hit.astype(jnp.int32)
    for meta, count, out_ref in zip(metas, used, out_refs):
        meta = jnp.where(lane == USED_AT, count.astype(jnp.float32), meta)
        out_ref[out_ref.shape[0] - META :, :] = meta


def fetch_ids(parts, ids_ref, sems):
    copies = [
        pltpu.make_async_copy(ref.at[pl.ds(at, META), :], ids_ref.at[i], sems.at[i])
        for i, (ref, at) in enumerate(parts)
    ]
    for copy in copies:
        copy.start()

    def wait():
        for copy in copies:
            copy.wait()

    return wait


def id_scratch(groups):
    return [pltpu.SMEM((groups, META, LANES), jnp.float32), pltpu.SemaphoreType.DMA((groups,))]


def far_hops(plane):
    pair = (4 - 8 * (plane // 4 % 2)) * (1 - 2 * (plane % 2))
    return [pair, -pair]


def near_hops(plane):
    side = 2 * (plane % 2) - 1
    return [side, -side, 2 * side]


def metas(refs, rows=0):
    return [(ref, at + (rows or ref.shape[0]) - META) for ref in refs for at in range(0, ref.shape[0], rows or ref.shape[0])]


def blocks_of(refs, rows, block, ids_ref):
    items = []
    for i, (ref, end) in enumerate(metas(refs, rows)):
        for f in range((rows - META) // block):
            ids = [ids_ref[i, 0, lane + f].astype(jnp.int32) for lane in (OWNER_AT, DEST_AT)]
            items.append((ref, end + META - rows + f * block, *ids))
    return items


def join_kernel(first_ref, second_ref, out_ref):
    rows = first_ref.shape[0]
    out_ref[:rows, :] = first_ref[...]
    out_ref[rows:, :] = second_ref[...]


def relay_kernel(*refs, rows, block):
    held, out_refs, ids_ref, sems = refs[:2], refs[2:-2], refs[-2], refs[-1]
    fetch_ids(metas(held, rows), ids_ref, sems)()
    me = lax.axis_index("pitch")
    count = lax.axis_size("pitch")
    halo = held[0][rows - META : rows, :]
    items = blocks_of(held, rows, block, ids_ref)
    targets = [lax.rem(me + count + by, count) for by in near_hops(me)]
    route(items, targets, halo, block, out_refs)


def add_block(out_ref, ref, at, dest):
    nvars = out_ref.shape[0]
    to = pl.ds(pl.multiple_of(dest * LANES, LANES), LANES)
    for v in range(nvars):
        out_ref[v, :, to] += ref[pl.ds(pl.multiple_of(at + v * ROWS, ROWS), ROWS), :]


def base_kernel(flow_ref, speed_ref, first_ref, second_ref, *refs, rows):
    held, out_ref, ids_ref, sems = refs[:2], refs[-3], refs[-2], refs[-1]
    wait = fetch_ids(metas(held, rows), ids_ref, sems)
    nvars, _, cells = flow_ref.shape
    block = nvars * ROWS
    per = cells // LANES
    me = lax.axis_index("pitch")
    lane = lax.broadcasted_iota(jnp.int32, (ROWS, LANES), 1)
    first, second = [ref[ref.shape[0] - META :, :] for ref in (first_ref, second_ref)]
    odd = lax.rem(me, 2) == 1
    before, after = jnp.where(odd, second, first), jnp.where(odd, first, second)
    for v in range(nvars):
        left_edge = pltpu.roll(before, (LANES - v) % LANES, 1)
        right_edge = pltpu.roll(after, LANES - 1 - nvars - v, 1)
        tiles = [flow_ref[v, :, c * LANES : (c + 1) * LANES] for c in range(per)]
        downs = [pltpu.roll(tile, 1, 1) for tile in tiles]
        ups = [pltpu.roll(tile, LANES - 1, 1) for tile in tiles]
        for c in range(per):
            down = jnp.where(lane == 0, left_edge if c == 0 else downs[c - 1], downs[c])
            up = jnp.where(lane == LANES - 1, right_edge if c == per - 1 else ups[c + 1], ups[c])
            speed = speed_ref[c : c + 1, :]
            out_ref[v, :, c * LANES : (c + 1) * LANES] = -speed * (up - down) * 0.5
    wait()
    items = blocks_of(held, rows, block, ids_ref)
    for ref, at, owner, dest in items:

        @pl.when(owner == me)
        def _(ref=ref, at=at, dest=dest):
            add_block(out_ref, ref, at, dest)


def spectral_matrix(count):
    column = lax.broadcasted_iota(jnp.int32, (ROWS, count), 1)
    gap = (count - column) % count
    safe = jnp.where(gap == 0, 1, gap).astype(jnp.float32)
    angle = jnp.float32(jnp.pi) * safe / count
    parity = (1 - 2 * (gap % 2)).astype(jnp.float32)
    value = jnp.float32(jnp.pi) / count * parity * jnp.cos(angle) / jnp.sin(angle)
    row = jnp.where(gap == 0, jnp.float32(0.0), value)
    return pltpu.roll(jnp.broadcast_to(row[:1], (count, count)), 0, 1, stride=1, stride_axis=0)


def spectral_kernel(cells_ref, out_ref, *, count, first_mean, last_mean):
    devs = count // ROWS
    slots = cells_ref.shape[0] // count
    me = lax.axis_index("tm")
    got = cells_ref[...].reshape(devs, slots, ROWS, LANES)
    columns = jnp.concatenate([got[:, k].reshape(count, LANES) for k in range(slots)], axis=1)
    product = jnp.dot(
        spectral_matrix(count), columns, precision=lax.Precision.HIGHEST, preferred_element_type=jnp.float32
    )
    for k in range(slots):
        tile = me * slots + k
        is_mean = jnp.logical_and(tile >= first_mean, tile < last_mean)
        mean = jnp.sum(got[:, k], axis=0) / count
        for d in range(devs):
            part = product[d * ROWS : (d + 1) * ROWS, k * LANES : (k + 1) * LANES]
            at = (d * slots + k) * ROWS
            out_ref[at : at + ROWS, :] = jnp.where(is_mean, mean, part)


def finish_kernel(*refs):
    base_ref, cells_ref, blocks = refs[0], refs[1], refs[2:-4]
    out_ref, mean_ref, ids_ref, sems = refs[-4:]
    wait = fetch_ids(metas(blocks), ids_ref, sems)
    nvars, _, cells = out_ref.shape
    block = nvars * ROWS
    per = cells // LANES
    for m in range(nvars * per):
        v, c = divmod(m, per)
        at = slice(c * LANES, (c + 1) * LANES)
        out_ref[v, :, at] = cells_ref[m * ROWS : (m + 1) * ROWS, :] + base_ref[v, :, at]
        row = nvars * per * ROWS + m
        mean_ref[v : v + 1, at] = cells_ref[row : row + 1, :]
    wait()
    for i, ref in enumerate(blocks):

        def add(slot, carry, i=i, ref=ref):
            add_block(out_ref, ref, slot * block, ids_ref[i, 0, DEST_AT + slot].astype(jnp.int32))
            return carry

        lax.fori_loop(0, ids_ref[i, 0, USED_AT].astype(jnp.int32), add, 0)


def sent_by(array, hops, i):
    count = lax.axis_size("pitch")
    return lax.ppermute(array, "pitch", [(p, (p + hops(p)[i]) % count) for p in range(count)])


def per_device(flow, speed, rotor_face, owner, dest_block, intersection):
    nvars, inst, cells = flow.shape
    faces = rotor_face.shape[1]
    devs = lax.axis_size("tm")
    count = inst * devs
    block = nvars * inst
    tiles = nvars * cells // LANES
    slots = -(-(tiles + tiles // ROWS) // devs)
    owner, dest_block, intersection = [a.reshape(1, faces) for a in (owner, dest_block, intersection)]
    rotor = jnp.transpose(rotor_face, (0, 2, 1, 3)).reshape(inst * nvars * faces, LANES)
    speed = speed.reshape(cells // LANES, LANES)

    operands = (flow, rotor, owner, dest_block, intersection)
    packed, mine = call(
        prepare_kernel,
        (f32(devs * slots * ROWS, LANES), f32(faces * block + META, LANES)),
        [pl.BlockSpec(memory_space=pl.ANY)] * IN,
        [pltpu.VMEM(a.shape, a.dtype) for a in operands] + [pltpu.SemaphoreType.DMA((nvars + IN - 1,))],
        moved=1_200_000,
        room=ALL_VMEM,
    )(*operands)
    by_cell = lax.all_to_all(packed, "tm", 0, 0, tiled=True)
    product = call(
        functools.partial(spectral_kernel, count=count, first_mean=tiles, last_mean=tiles + tiles // ROWS),
        f32(devs * slots * ROWS, LANES),
        [vmem()],
        flops=6 * 2 * count * count * slots * LANES,
        moved=1_000_000,
    )(by_cell)
    rows = mine.shape[0]
    both = call(join_kernel, f32(2 * rows, LANES), [vmem()] * 2, flops=SLOW, moved=500_000)(mine, sent_by(mine, far_hops, 0))
    held = [both, sent_by(both, far_hops, 1)]
    planes = 2 * len(held)
    relays = call(
        functools.partial(relay_kernel, rows=rows, block=block),
        [f32(planes * CAP * block + META, LANES) for _ in range(NEAR)],
        [vmem()] * len(held),
        id_scratch(planes),
        flops=20000000000,
        moved=1_500_000,
    )(*held)
    sent = [sent_by(a, near_hops, i) for i, a in enumerate(relays)]
    base = call(
        functools.partial(base_kernel, rows=rows),
        f32(nvars, inst, cells),
        [vmem()] * (4 + len(held)),
        id_scratch(planes),
        moved=900_000,
    )(flow, speed, sent[0], sent[1], *held)

    by_time = lax.all_to_all(product, "tm", 0, 0, tiled=True)
    residual, mean_flow = call(
        finish_kernel,
        (f32(nvars, inst, cells), f32(nvars, cells)),
        [vmem()] * (2 + len(sent)),
        id_scratch(len(sent)),
        moved=1_500_000,
    )(base, by_time, *sent)
    return residual, mean_flow


def solution(mesh):
    placed = (
        P(None, "tm", "pitch"),
        P("pitch"),
        P("tm", "pitch", None, None),
        P("pitch", None),
        P("pitch"),
        P("pitch"),
    )
    return jax.shard_map(
        per_device,
        mesh=mesh,
        in_specs=placed,
        out_specs=(P(None, "tm", "pitch"), P(None, "pitch")),
        check_vma=False,
    )
```

```python
import functools

import jax
import jax.numpy as jnp
from jax import lax
from jax.experimental import pallas as pl
from jax.experimental.pallas import tpu as pltpu
from jax.sharding import PartitionSpec as P

LANES = 128
ROWS = 8
META = 8
OWNER_AT, DEST_AT, USED_AT = 16, 24, 40
VMEM = 32 * 1024 * 1024
ALL_VMEM = 60 * 1024 * 1024
IN = 5
SLOW = 20_000_000_000
CAP = 2
NEAR = 3


def vmem():
    return pl.BlockSpec(memory_space=pltpu.VMEM)


def smem():
    return pl.BlockSpec(memory_space=pltpu.SMEM)


def call(body, outs, in_specs, scratch=(), flops=0, moved=0, room=VMEM):
    return pl.pallas_call(
        body,
        out_shape=outs,
        in_specs=in_specs,
        out_specs=jax.tree.map(lambda _: vmem(), outs),
        scratch_shapes=list(scratch),
        compiler_params=pltpu.CompilerParams(vmem_limit_bytes=room),
        cost_estimate=pl.CostEstimate(flops=flops, bytes_accessed=moved, transcendentals=0),
    )


def f32(*shape):
    return jax.ShapeDtypeStruct(shape, jnp.float32)


def prepare_kernel(*refs):
    given, (packed_ref, mine_ref), held, sems = refs[:IN], refs[IN : IN + 2], refs[IN + 2 : -1], refs[-1]
    flow_ref, rotor_ref, owner_ref, dest_ref, weight_ref = held
    nvars = flow_ref.shape[0]
    flows = [pltpu.make_async_copy(given[0].at[v], flow_ref.at[v], sems.at[v]) for v in range(nvars)]
    rest = [pltpu.make_async_copy(given[i], held[i], sems.at[nvars - 1 + i]) for i in range(1, IN)]
    for copy in flows + rest:
        copy.start()
    pack(flows, flow_ref, packed_ref)
    for copy in rest:
        copy.wait()
    weigh(owner_ref, dest_ref, weight_ref, flow_ref, rotor_ref, mine_ref)


def pack(copies, flow_ref, out_ref):
    nvars, _, cells = flow_ref.shape
    per = cells // LANES
    tiles = nvars * per
    row = lax.broadcasted_iota(jnp.int32, (ROWS, LANES), 0)
    sums = None
    for m in range(tiles):
        v, c = divmod(m, per)
        if c == 0:
            copies[v].wait()
        tile = flow_ref[v, :, c * LANES : (c + 1) * LANES]
        out_ref[m * ROWS : (m + 1) * ROWS, :] = tile
        total = jnp.sum(tile, axis=0, keepdims=True)
        total = jnp.broadcast_to(total, (ROWS, LANES))
        sums = total if m % ROWS == 0 else jnp.where(row == m % ROWS, total, sums)
        if m % ROWS == ROWS - 1:
            q = tiles + m // ROWS
            out_ref[q * ROWS : (q + 1) * ROWS, :] = sums
    used = (tiles + tiles // ROWS) * ROWS
    out_ref[used:, :] = jnp.zeros((out_ref.shape[0] - used, LANES), jnp.float32)


def weigh(owner_ref, dest_ref, weight_ref, flow_ref, rotor_ref, mine_ref):
    nvars, _, cells = flow_ref.shape
    faces = weight_ref.shape[1]
    block = nvars * ROWS
    lane = lax.broadcasted_iota(jnp.int32, (ROWS, LANES), 1)
    meta = jnp.zeros((ROWS, LANES), jnp.float32)
    for v in range(nvars):
        tail = pltpu.roll(flow_ref[v, :, cells - LANES :], v + 1, 1)
        head = pltpu.roll(flow_ref[v, :, :LANES], nvars + v, 1)
        meta = jnp.where(lane == v, tail, meta)
        meta = jnp.where(lane == nvars + v, head, meta)
    for f in range(faces):
        own = slice(f, f + 1)
        weight = jnp.broadcast_to(weight_ref[:, own], (ROWS, LANES))
        for at, ref in ((OWNER_AT, owner_ref), (DEST_AT, dest_ref)):
            meta = jnp.where(lane == at + f, ref[:, own].astype(jnp.float32), meta)
        for v in range(nvars):
            rows = rotor_ref[pl.ds(v * faces + f, ROWS, stride=nvars * faces), :]
            at = f * block + v * ROWS
            mine_ref[at : at + ROWS, :] = weight * rows
    mine_ref[faces * block :, :] = meta


def route(items, targets, halo, block, out_refs):
    lane = lax.broadcasted_iota(jnp.int32, (META, LANES), 1)
    metas = [jnp.where(lane < OWNER_AT, halo, -1.0) for _ in targets]
    used = [jnp.int32(0) for _ in targets]
    for ref, at, owner, dest in items:
        hits = [owner == target for target in targets]

        @pl.when(functools.reduce(jnp.logical_or, hits))
        def _(ref=ref, at=at, hits=hits, used=tuple(used)):
            for hit, slot, out_ref in zip(hits, used, out_refs):

                @pl.when(hit)
                def _(slot=slot, out_ref=out_ref):
                    to = pl.multiple_of(slot * block, block)
                    out_ref[pl.ds(to, block), :] = ref[at : at + block, :]

        for i, hit in enumerate(hits):
            where = jnp.where(hit, DEST_AT + used[i], -1)
            metas[i] = jnp.where(lane == where, dest.astype(jnp.float32), metas[i])
            used[i] = used[i] + hit.astype(jnp.int32)
    for meta, count, out_ref in zip(metas, used, out_refs):
        meta = jnp.where(lane == USED_AT, count.astype(jnp.float32), meta)
        out_ref[out_ref.shape[0] - META :, :] = meta


def fetch_ids(parts, ids_ref, sems):
    copies = [
        pltpu.make_async_copy(ref.at[pl.ds(at, META), :], ids_ref.at[i], sems.at[i])
        for i, (ref, at) in enumerate(parts)
    ]
    for copy in copies:
        copy.start()

    def wait():
        for copy in copies:
            copy.wait()

    return wait


def id_scratch(groups):
    return [pltpu.SMEM((groups, META, LANES), jnp.float32), pltpu.SemaphoreType.DMA((groups,))]


def far_hops(plane):
    pair = (4 - 8 * (plane // 4 % 2)) * (1 - 2 * (plane % 2))
    return [pair, -pair]


def near_hops(plane):
    side = 2 * (plane % 2) - 1
    return [side, -side, 2 * side]


def metas(refs, rows=0):
    return [(ref, at + (rows or ref.shape[0]) - META) for ref in refs for at in range(0, ref.shape[0], rows or ref.shape[0])]


def blocks_of(refs, rows, block, ids_ref):
    items = []
    for i, (ref, end) in enumerate(metas(refs, rows)):
        for f in range((rows - META) // block):
            ids = [ids_ref[i, 0, lane + f].astype(jnp.int32) for lane in (OWNER_AT, DEST_AT)]
            items.append((ref, end + META - rows + f * block, *ids))
    return items


def join_kernel(first_ref, second_ref, out_ref):
    rows = first_ref.shape[0]
    out_ref[:rows, :] = first_ref[...]
    out_ref[rows:, :] = second_ref[...]


def relay_kernel(*refs, rows, block):
    held, out_refs, ids_ref, sems = refs[:2], refs[2:-2], refs[-2], refs[-1]
    fetch_ids(metas(held, rows), ids_ref, sems)()
    me = lax.axis_index("pitch")
    count = lax.axis_size("pitch")
    halo = held[0][rows - META : rows, :]
    items = blocks_of(held, rows, block, ids_ref)
    targets = [lax.rem(me + count + by, count) for by in near_hops(me)]
    route(items, targets, halo, block, out_refs)


def add_block(out_ref, ref, at, dest):
    nvars = out_ref.shape[0]
    to = pl.ds(pl.multiple_of(dest * LANES, LANES), LANES)
    for v in range(nvars):
        out_ref[v, :, to] += ref[pl.ds(pl.multiple_of(at + v * ROWS, ROWS), ROWS), :]


def base_kernel(flow_ref, speed_ref, out_ref):
    nvars, _, cells = flow_ref.shape
    per = cells // LANES
    lane = lax.broadcasted_iota(jnp.int32, (ROWS, LANES), 1)
    edge = jnp.zeros((ROWS, LANES), jnp.float32)
    for v in range(nvars):
        tiles = [flow_ref[v, :, c * LANES : (c + 1) * LANES] for c in range(per)]
        downs = [pltpu.roll(tile, 1, 1) for tile in tiles]
        ups = [pltpu.roll(tile, LANES - 1, 1) for tile in tiles]
        for c in range(per):
            down = jnp.where(lane == 0, edge if c == 0 else downs[c - 1], downs[c])
            up = jnp.where(lane == LANES - 1, edge if c == per - 1 else ups[c + 1], ups[c])
            out_ref[v, :, c * LANES : (c + 1) * LANES] = -speed_ref[c : c + 1, :] * (up - down) * 0.5


def add_edges(out_ref, speed_ref, first, second):
    nvars, _, cells = out_ref.shape
    lane = lax.broadcasted_iota(jnp.int32, (ROWS, LANES), 1)
    odd = lax.rem(lax.axis_index("pitch"), 2) == 1
    before, after = jnp.where(odd, second, first), jnp.where(odd, first, second)
    last = cells // LANES - 1
    for v in range(nvars):
        left = pltpu.roll(before, (LANES - v) % LANES, 1)
        right = pltpu.roll(after, LANES - 1 - nvars - v, 1)
        out_ref[v, :, :LANES] += jnp.where(lane == 0, speed_ref[:1, :] * left * 0.5, 0.0)
        out_ref[v, :, cells - LANES :] += jnp.where(lane == LANES - 1, -speed_ref[last:, :] * right * 0.5, 0.0)


def spectral_matrix(count):
    column = lax.broadcasted_iota(jnp.int32, (ROWS, count), 1)
    gap = (count - column) % count
    safe = jnp.where(gap == 0, 1, gap).astype(jnp.float32)
    angle = jnp.float32(jnp.pi) * safe / count
    parity = (1 - 2 * (gap % 2)).astype(jnp.float32)
    value = jnp.float32(jnp.pi) / count * parity * jnp.cos(angle) / jnp.sin(angle)
    row = jnp.where(gap == 0, jnp.float32(0.0), value)
    return pltpu.roll(jnp.broadcast_to(row[:1], (count, count)), 0, 1, stride=1, stride_axis=0)


def spectral_kernel(cells_ref, out_ref, *, count, first_mean, last_mean):
    devs = count // ROWS
    slots = cells_ref.shape[0] // count
    me = lax.axis_index("tm")
    got = cells_ref[...].reshape(devs, slots, ROWS, LANES)
    columns = jnp.concatenate([got[:, k].reshape(count, LANES) for k in range(slots)], axis=1)
    product = jnp.dot(
        spectral_matrix(count), columns, precision=lax.Precision.HIGHEST, preferred_element_type=jnp.float32
    )
    for k in range(slots):
        tile = me * slots + k
        is_mean = jnp.logical_and(tile >= first_mean, tile < last_mean)
        mean = jnp.sum(got[:, k], axis=0) / count
        for d in range(devs):
            part = product[d * ROWS : (d + 1) * ROWS, k * LANES : (k + 1) * LANES]
            at = (d * slots + k) * ROWS
            out_ref[at : at + ROWS, :] = jnp.where(is_mean, mean, part)


def finish_kernel(*refs, rows):
    base_ref, cells_ref, speed_ref, held, blocks = refs[0], refs[1], refs[2], refs[3:5], refs[5:-4]
    out_ref, mean_ref, ids_ref, sems = refs[-4:]
    wait = fetch_ids(metas(blocks) + metas(held, rows), ids_ref, sems)
    nvars, _, cells = out_ref.shape
    block = nvars * ROWS
    per = cells // LANES
    for m in range(nvars * per):
        v, c = divmod(m, per)
        at = slice(c * LANES, (c + 1) * LANES)
        out_ref[v, :, at] = cells_ref[m * ROWS : (m + 1) * ROWS, :] + base_ref[v, :, at]
        row = nvars * per * ROWS + m
        mean_ref[v : v + 1, at] = cells_ref[row : row + 1, :]
    add_edges(out_ref, speed_ref, *[ref[ref.shape[0] - META :, :] for ref in blocks[:2]])
    wait()
    me = lax.axis_index("pitch")
    for ref, at, owner, dest in blocks_of(held, rows, block, ids_ref.at[pl.ds(NEAR, ids_ref.shape[0] - NEAR)]):

        @pl.when(owner == me)
        def _(ref=ref, at=at, dest=dest):
            add_block(out_ref, ref, at, dest)

    for i, ref in enumerate(blocks):

        def add(slot, carry, i=i, ref=ref):
            add_block(out_ref, ref, slot * block, ids_ref[i, 0, DEST_AT + slot].astype(jnp.int32))
            return carry

        lax.fori_loop(0, ids_ref[i, 0, USED_AT].astype(jnp.int32), add, 0)


def sent_by(array, hops, i):
    count = lax.axis_size("pitch")
    return lax.ppermute(array, "pitch", [(p, (p + hops(p)[i]) % count) for p in range(count)])


def per_device(flow, speed, rotor_face, owner, dest_block, intersection):
    nvars, inst, cells = flow.shape
    faces = rotor_face.shape[1]
    devs = lax.axis_size("tm")
    count = inst * devs
    block = nvars * inst
    tiles = nvars * cells // LANES
    slots = -(-(tiles + tiles // ROWS) // devs)
    owner, dest_block, intersection = [a.reshape(1, faces) for a in (owner, dest_block, intersection)]
    rotor = jnp.transpose(rotor_face, (0, 2, 1, 3)).reshape(inst * nvars * faces, LANES)
    speed = speed.reshape(cells // LANES, LANES)

    operands = (flow, rotor, owner, dest_block, intersection)
    packed, mine = call(
        prepare_kernel,
        (f32(devs * slots * ROWS, LANES), f32(faces * block + META, LANES)),
        [pl.BlockSpec(memory_space=pl.ANY)] * IN,
        [pltpu.VMEM(a.shape, a.dtype) for a in operands] + [pltpu.SemaphoreType.DMA((nvars + IN - 1,))],
        moved=1_200_000,
        room=ALL_VMEM,
    )(*operands)
    by_cell = lax.all_to_all(packed, "tm", 0, 0, tiled=True)
    product = call(
        functools.partial(spectral_kernel, count=count, first_mean=tiles, last_mean=tiles + tiles // ROWS),
        f32(devs * slots * ROWS, LANES),
        [vmem()],
        flops=6 * 2 * count * count * slots * LANES,
        moved=1_000_000,
    )(by_cell)
    rows = mine.shape[0]
    both = call(join_kernel, f32(2 * rows, LANES), [vmem()] * 2, flops=SLOW, moved=500_000)(mine, sent_by(mine, far_hops, 0))
    held = [both, sent_by(both, far_hops, 1)]
    planes = 2 * len(held)
    relays = call(
        functools.partial(relay_kernel, rows=rows, block=block),
        [f32(planes * CAP * block + META, LANES) for _ in range(NEAR)],
        [vmem()] * len(held),
        id_scratch(planes),
        flops=20000000000,
        moved=1_500_000,
    )(*held)
    sent = [sent_by(a, near_hops, i) for i, a in enumerate(relays)]
    base = call(base_kernel, f32(nvars, inst, cells), [vmem()] * 2, moved=900_000)(flow, speed)
    by_time = lax.all_to_all(product, "tm", 0, 0, tiled=True)
    residual, mean_flow = call(
        functools.partial(finish_kernel, rows=rows),
        (f32(nvars, inst, cells), f32(nvars, cells)),
        [vmem()] * (5 + len(sent)),
        id_scratch(planes + len(sent)),
        moved=1_500_000,
    )(base, by_time, speed, *held, *sent)
    return residual, mean_flow


def solution(mesh):
    placed = (
        P(None, "tm", "pitch"),
        P("pitch"),
        P("tm", "pitch", None, None),
        P("pitch", None),
        P("pitch"),
        P("pitch"),
    )
    return jax.shard_map(
        per_device,
        mesh=mesh,
        in_specs=placed,
        out_specs=(P(None, "tm", "pitch"), P(None, "pitch")),
        check_vma=False,
    )
```
